32 devices in a mesh: gx: 4 (over y, x), gy: 8 (over z, core).
Axes of the slice: x: 2, y: 2, z: 4, core: 2. Of those that a mesh axis runs over, the one named last changes fastest.
Arguments:
- right_side: float32 [16384, 64], P(('gx', 'gy')), may hold values from -6 to 6
- leaf_inverse: float32 [16384, 512], P(('gx', 'gy')), as said below
- basis_one: float32 [16384, 128], P(('gx', 'gy')), may hold values from -0.0625 to 0.0625
- basis_two: float32 [16384, 128], P(('gx', 'gy')), may hold values from -0.09375 to 0.09375
- factor_one: bfloat16 [1, 256, 256], replicated, may hold values from -0.5 to 0.5
- factor_two: bfloat16 [2, 256, 256], replicated, may hold values from -0.5 to 0.5
Outputs:
- solution: float32 [16384, 64], P(('gx', 'gy'))
The draws below stay inside these ranges and needn't reach their ends.
Inputs may be any that keep to these rules, and one draw needn't show every extreme that they name: `leaf_inverse`: each block of 512 consecutive rows is a symmetric positive definite 512 x 512 matrix.
All inputs are finite; a program needn't handle non-finite values.
Results may differ from the reference program's by a relative error of at most 0.0003.
Values sent between devices are 32-bit elements; how exact they have to be, the bound alone decides.
No kernel may reach another device: no remote copies, remote signals or barrier semaphores. Data moves between devices by JAX's collectives and lax.ppermute only.
A program may use at most 64 MiB of HBM per device.

```python
import jax
import jax.numpy as jnp
from jax import lax

LEAF = 512
R = 128
NRHS = 64
LEVELS = 2
NROWS = 16384


def draw_leaf_inverse(key, part):
    block_count = NROWS // LEAF
    inner = LEAF // 4
    first, second = jax.random.split(jax.random.fold_in(key, 11))
    mixing = jax.random.normal(first, (block_count, LEAF, inner), jnp.float32)
    scales = jnp.exp(jax.random.uniform(second, (block_count, LEAF), jnp.float32, -0.3, 0.3))
    core = jnp.einsum('bik,bjk->bij', mixing, mixing) / inner + 0.5 * jnp.eye(LEAF, dtype=jnp.float32)
    scaled = scales[:, :, None] * core * scales[:, None, :]
    return scaled.reshape(NROWS, LEAF).astype(jnp.float32)


def block_scale(key, extent, pieces, least, high):
    factor_of = 1.0
    for axis_at, blocks in pieces:
        heights = jax.random.uniform(jax.random.fold_in(jax.random.fold_in(key, 6), axis_at), (blocks,), jnp.float32, least / len(pieces), high / len(pieces))
        factor_of = factor_of * jnp.repeat(jnp.exp(heights), extent[axis_at] // blocks).reshape((-1,) + (1,) * (len(extent) - 1 - axis_at))
    return factor_of


def centred(rng, dims, scale, bound, cuts=(), kind=jnp.bfloat16):
    result = scale * jax.random.normal(rng, dims, jnp.float32)
    if cuts:
        result = result * block_scale(rng, dims, cuts, -0.22, 0.18)
    return jnp.clip(result, -bound, bound).astype(kind)


def setup_inputs(seed: int = 0) -> dict:
    splits = jax.random.split(jax.random.key(seed), 7)
    return {
        "right_side": centred(splits[0], (NROWS, NRHS), 1.0, 6.0, ((0, 32),), jnp.float32),
        "leaf_inverse": draw_leaf_inverse(jax.random.fold_in(splits[6], 71), 0),
        "basis_one": centred(splits[2], (NROWS, R), (NROWS // 2) ** -0.5, 0.0625, ((0, 32),), jnp.float32),
        "basis_two": centred(splits[3], (NROWS, R), (NROWS // 4) ** -0.5, 0.09375, ((0, 32),), jnp.float32),
        "factor_one": centred(splits[4], (1, 2 * R, 2 * R), R ** -0.5, 0.5),
        "factor_two": centred(splits[5], (2, 2 * R, 2 * R), R ** -0.5, 0.5),
    }


HIGH = lax.Precision.HIGHEST

def solve_small(matrix, right_terms):
    lower_factor = jnp.linalg.cholesky(matrix)
    middle = lax.linalg.triangular_solve(lower_factor, right_terms, left_side=True, lower=True)
    return lax.linalg.triangular_solve(lower_factor, middle, left_side=True, lower=True, transpose_a=True)

def reference(right_side, leaf_inverse, basis_one, basis_two, factor_one, factor_two):
    level_bases = (basis_one, basis_two)
    factors = (factor_one, factor_two)
    block_count = NROWS // LEAF
    stacked = jnp.concatenate((right_side,) + level_bases, axis=1).reshape(block_count, LEAF, -1)
    current = jnp.einsum('bij,bjc->bic', leaf_inverse.reshape(block_count, LEAF, LEAF), stacked, precision=HIGH)
    identity = jnp.eye(2 * R, dtype=jnp.float32)
    for level_index in range(LEVELS, 0, -1):
        width_used = NRHS + (level_index - 1) * R
        group_count = 2 ** level_index
        remaining = current[:, :, :width_used].reshape(group_count, -1, width_used)
        solved = current[:, :, width_used:width_used + R].reshape(group_count, -1, R)
        basis_rows = level_bases[level_index - 1].reshape(group_count, -1, R)
        gram_local = jnp.einsum('bnr,bns->brs', basis_rows, solved, precision=HIGH)
        projection = jnp.einsum('bnr,bnc->brc', basis_rows, remaining, precision=HIGH)
        factor = factors[level_index - 1].astype(jnp.float32).reshape(group_count // 2, 2, R, 2 * R)
        gram_pairs = gram_local.reshape(group_count // 2, 2, R, R)
        capacitance = identity + jnp.einsum('phra,phrs,phsb->pab', factor, gram_pairs, factor, precision=HIGH)
        right_terms = jnp.einsum('phra,phrc->pac', factor, projection.reshape(group_count // 2, 2, R, width_used), precision=HIGH)
        coefficient = solve_small(capacitance, right_terms)
        update = jnp.einsum('phra,pac->phrc', factor, coefficient, precision=HIGH).reshape(group_count, R, width_used)
        remaining = remaining - jnp.einsum('bnr,brc->bnc', solved, update, precision=HIGH)
        current = remaining.reshape(block_count, LEAF, width_used)
    return current.reshape(NROWS, NRHS)
```

```python
import jax
import jax.numpy as jnp
from jax import lax
from jax.experimental import pallas as pl
from jax.experimental.pallas import tpu as pltpu
from jax.sharding import PartitionSpec as P

HIGH = lax.Precision.HIGHEST
F32 = jnp.float32
SUB = 8
VMEM_BYTES = 32 * 1024 * 1024


def partner(value, axis, mask):
    pairs = [(source, source ^ mask) for source in range(lax.axis_size(axis))]
    return lax.ppermute(value, axis, pairs)


def matmul(left, right):
    return jnp.dot(left, right, precision=HIGH, preferred_element_type=F32)


def matmul_tn(left, right):
    return lax.dot_general(
        left, right, (((0,), (0,)), ((), ())), precision=HIGH, preferred_element_type=F32
    )


def sweep_block(elements):
    e = [list(row) for row in elements]

    def get(i, j):
        return e[i][j] if i >= j else e[j][i]

    for t in range(SUB):
        scale = 1.0 / e[t][t]
        old = [get(i, t) for i in range(SUB)]
        new = [old[i] * scale for i in range(SUB)]
        for i in range(SUB):
            for j in range(i + 1):
                if i != t and j != t:
                    e[i][j] = e[i][j] - new[i] * old[j]
        for i in range(SUB):
            if i > t:
                e[i][t] = new[i]
            elif i < t:
                e[t][i] = new[i]
        e[t][t] = -scale
    return get


def inverse_spd(matrix):
    order = matrix.shape[0]
    panel = (SUB, order)
    row_at = lax.broadcasted_iota(jnp.int32, panel, 0)
    lane_at = lax.broadcasted_iota(jnp.int32, panel, 1)
    rows = [matrix[SUB * i : SUB * (i + 1), :] for i in range(order // SUB)]
    for k in range(order // SUB):
        base = SUB * k
        pivot_row = rows[k]
        columns = [
            jnp.broadcast_to(pivot_row[:, base + j : base + j + 1], panel) for j in range(SUB)
        ]
        get = sweep_block(
            [
                [jnp.broadcast_to(columns[j][i : i + 1, :], panel) for j in range(i + 1)]
                for i in range(SUB)
            ]
        )
        inside = (lane_at >= base) & (lane_at < base + SUB)
        unit = jnp.where(lane_at - base == row_at, 1.0, 0.0)
        pivot_row = jnp.where(inside, unit, pivot_row)
        scaled = None
        for j in range(SUB):
            column = get(SUB - 1, j)
            for i in range(SUB - 2, -1, -1):
                column = jnp.where(row_at == i, get(i, j), column)
            term = column * jnp.broadcast_to(pivot_row[j : j + 1, :], panel)
            scaled = term if scaled is None else scaled + term
        spread = [jnp.broadcast_to(scaled[j : j + 1, :], panel) for j in range(SUB)]
        for i in range(order // SUB):
            if i == k:
                continue
            total = jnp.where(inside, 0.0, rows[i])
            for j in range(SUB):
                column = jnp.broadcast_to(rows[i][:, base + j : base + j + 1], panel)
                total = total + column * spread[j]
            rows[i] = total
        rows[k] = -scaled
    return jnp.concatenate(rows, axis=0)


def solve_spd(system, rank):
    first, second = system[:rank], system[rank:]
    head = matmul(inverse_spd(first[:, :rank]), first[:, rank:])
    rest = second[:, rank:] - matmul(second[:, :rank], head)
    low = matmul(inverse_spd(rest[:, :rank]), rest[:, rank:])
    high = head[:, rank:] - matmul(head[:, :rank], low)
    return jnp.concatenate((high, low), axis=0)


def add_eye(system):
    row_at = lax.broadcasted_iota(jnp.int32, system.shape, 0)
    lane_at = lax.broadcasted_iota(jnp.int32, system.shape, 1)
    return system + jnp.where(row_at == lane_at, 1.0, 0.0)


def local_kernel(rhs_ref, leaf_ref, one_ref, two_ref, solved_ref, keep_ref, give_ref):
    rank = one_ref.shape[1]
    width = rhs_ref.shape[1]
    bases = jnp.concatenate((two_ref[...], one_ref[...]), axis=1)
    solved = matmul(leaf_ref[...], jnp.concatenate((bases, rhs_ref[...]), axis=1))
    solved_ref[...] = solved
    products = matmul_tn(bases, solved)
    g22 = products[:rank, :rank]
    g21 = products[:rank, rank : 2 * rank]
    g11 = products[rank:, rank : 2 * rank]
    row_at = lax.broadcasted_iota(jnp.int32, (rank, rank), 0)
    lane_at = lax.broadcasted_iota(jnp.int32, (rank, rank), 1)
    both = jnp.where(row_at >= lane_at, g22, g11)
    diagonal = jnp.sum(jnp.where(row_at == lane_at, g11, 0.0), axis=0, keepdims=True)
    terms = jnp.concatenate((products[:rank, 2 * rank :], products[rank:, 2 * rank :]), axis=1)
    half = keep_ref.shape[0] - SUB
    cut = half - rank
    pad = jnp.broadcast_to(diagonal, (SUB, rank))
    low = jnp.concatenate((both, terms[:cut], pad), axis=0)
    high = jnp.concatenate((g21, terms[cut:], pad), axis=0)
    upper = lax.axis_index("gy") % 2 == 1
    keep_ref[...] = jnp.where(upper, high, low)
    give_ref[...] = jnp.where(upper, low, high)


def unpack(low, high, rank):
    cut = rank // 2
    row_at = lax.broadcasted_iota(jnp.int32, (rank, rank), 0)
    lane_at = lax.broadcasted_iota(jnp.int32, (rank, rank), 1)
    both = low[:rank]
    flipped = both.T
    terms = jnp.concatenate((low[rank : rank + cut], high[rank : rank + cut]), axis=0)
    diagonal = jnp.broadcast_to(low[rank + cut : rank + cut + 1], (rank, rank))
    g22 = jnp.where(row_at >= lane_at, both, flipped)
    g11 = jnp.where(
        row_at < lane_at, both, jnp.where(row_at == lane_at, diagonal, flipped)
    )
    g21 = high[:rank]
    return g22, g21, g11, terms[:, : rank // 2], terms[:, rank // 2 :]


def second_kernel(mine_ref, other_ref, factor_ref, out_ref, update_ref):
    rank = factor_ref.shape[0] // 2
    upper = lax.axis_index("gy") % 2 == 1
    mine, other = mine_ref[...], other_ref[...]
    low = jnp.where(upper, other, mine)
    high = jnp.where(upper, mine, other)
    factor = factor_ref[...]
    g22, g21, g11, terms, later = [], [], [], [], []
    for side in range(2):
        parts = unpack(low[side], high[side], rank)
        g22.append(parts[0])
        g21.append(parts[1])
        g11.append(parts[2])
        terms.append(parts[3])
        later.append(parts[4])
    wide = jnp.concatenate(
        [
            jnp.concatenate(
                (matmul(g22[side], factor[side * rank : (side + 1) * rank]), g21[side], terms[side]),
                axis=1,
            )
            for side in range(2)
        ],
        axis=0,
    )
    update = matmul(factor, solve_spd(add_eye(matmul_tn(factor, wide)), rank))
    update_ref[...] = update[:rank]
    start = jnp.concatenate((g11[0] + g11[1], later[0] + later[1]), axis=1)
    out_ref[...] = start - matmul_tn(jnp.concatenate(g21, axis=0), update)


def first_kernel(mine_ref, other_ref, factor_ref, update_ref, solved_ref, out_ref):
    rank = factor_ref.shape[0] // 2
    factor = factor_ref[...]
    wide = jnp.concatenate(
        [
            jnp.concatenate(
                (
                    matmul(ref[:, :rank], factor[side * rank : (side + 1) * rank]),
                    ref[:, rank:],
                ),
                axis=1,
            )
            for side, ref in enumerate((mine_ref, other_ref))
        ],
        axis=0,
    )
    solution_terms = solve_spd(add_eye(matmul_tn(factor, wide)), rank)
    outer = matmul(factor[:rank], solution_terms)
    inner = update_ref[:, rank:] - matmul(update_ref[:, :rank], outer)
    out_ref[...] = solved_ref[:, 2 * rank :] - matmul(
        solved_ref[:, : 2 * rank], jnp.concatenate((inner, outer), axis=0)
    )


def call(kernel, shapes, *args):
    return pl.pallas_call(
        kernel,
        out_shape=[jax.ShapeDtypeStruct(shape, F32) for shape in shapes],
        compiler_params=pltpu.CompilerParams(vmem_limit_bytes=VMEM_BYTES),
    )(*args)


def pick_factor(factor, flat_index, group_bits, rank):
    pair_index = flat_index // 2 ** (group_bits + 1)
    half_index = flat_index // 2**group_bits % 2
    chosen = lax.dynamic_index_in_dim(factor, pair_index, 0, keepdims=False).astype(F32)
    return jnp.where(half_index == 1, jnp.roll(chosen, rank, axis=0), chosen)


def body(right_side, leaf_inverse, basis_one, basis_two, factor_one, factor_two):
    rank = basis_one.shape[1]
    rows, width = right_side.shape
    fine_bits = lax.axis_size("gy").bit_length() - 1
    total_bits = fine_bits + lax.axis_size("gx").bit_length() - 1
    flat_index = lax.axis_index("gx") * lax.axis_size("gy") + lax.axis_index("gy")
    two_bits, one_bits = total_bits - 2, total_bits - 1
    half = rank + rank // 2 + SUB
    solved, keep, give = call(
        local_kernel,
        [(rows, 2 * rank + width), (half, rank), (half, rank)],
        right_side,
        leaf_inverse,
        basis_one,
        basis_two,
    )
    total = keep + partner(give, "gy", 1)
    for bit in range(1, fine_bits):
        total = total + partner(total, "gy", 2**bit)
    for bit in range(two_bits - fine_bits):
        total = total + partner(total, "gx", 2**bit)
    sibling = partner(total, "gx", 2 ** (two_bits - fine_bits))
    mine = jnp.stack((total, sibling))
    other = partner(mine, "gy", 1)
    products, update = call(
        second_kernel,
        [(rank, rank + width), (rank, rank + width)],
        mine,
        other,
        pick_factor(factor_two, flat_index, two_bits, rank),
    )
    others = partner(products, "gx", 2 ** (one_bits - fine_bits))
    (result,) = call(
        first_kernel,
        [(rows, width)],
        products,
        others,
        pick_factor(factor_one, flat_index, one_bits, rank),
        update,
        solved,
    )
    return result


def solution(mesh):
    split = P(("gx", "gy"), None)
    return jax.shard_map(
        body,
        mesh=mesh,
        in_specs=(split, split, split, split, P(), P()),
        out_specs=split,
        check_vma=False,
    )
```

```python
import jax
import jax.numpy as jnp
from jax import lax
from jax.experimental import pallas as pl
from jax.experimental.pallas import tpu as pltpu
from jax.sharding import PartitionSpec as P

F32 = jnp.float32
BF16 = jnp.bfloat16
SUB = 8
NEAR = 2
VMEM_BYTES = 32 * 1024 * 1024
LOCAL_VMEM_BYTES = 107 * 512 * 1024

NN = (((1,), (0,)), ((), ()))
NT = (((1,), (1,)), ((), ()))


def partner(value, axis, mask):
    pairs = [(source, source ^ mask) for source in range(lax.axis_size(axis))]
    return lax.ppermute(value, axis, pairs)


def single(left, right, dims=NN):
    return lax.dot_general(left, right, dims, preferred_element_type=F32)


def times_factor(value, factor, dims=NN):
    high, low = split_pair(value)
    return single(high, factor, dims) + single(low, factor, dims)


def factor_times(factor, value):
    high, low = split_pair(value)
    return single(factor, high) + single(factor, low)


def split_pair(value):
    high = value.astype(BF16)
    return high, (value - high.astype(F32)).astype(BF16)


def pair_matmul(left, right, dims=NN):
    return single(left[0], right[0], dims) + (
        single(left[0], right[1], dims) + single(left[1], right[0], dims)
    )


def matmul(left, right, dims=NN):
    return pair_matmul(split_pair(left), split_pair(right), dims)


def tree_sum(terms):
    terms = list(terms)
    while len(terms) > 1:
        terms = [
            terms[i] + terms[i + 1] if i + 1 < len(terms) else terms[i]
            for i in range(0, len(terms), 2)
        ]
    return terms[0]


def across(panel, lane):
    return jnp.broadcast_to(panel[:, lane : lane + 1], panel.shape)


def down(panel, row):
    return jnp.broadcast_to(panel[row : row + 1, :], panel.shape)


def sweep_columns(columns, row_at):
    columns = list(columns)
    for t in range(SUB):
        pivot = columns[t]
        scale = 1.0 / down(pivot, t)
        here = row_at == t
        for j in range(SUB):
            if j != t:
                weight = down(columns[j], t) * scale
                columns[j] = jnp.where(here, weight, columns[j] - pivot * weight)
        columns[t] = jnp.where(here, scale, -(pivot * scale))
    return columns


def inverse_spd(matrix):
    order = matrix.shape[0]
    count = order // SUB
    shape = (SUB, order)
    row_at = lax.broadcasted_iota(jnp.int32, shape, 0)
    lane_at = lax.broadcasted_iota(jnp.int32, shape, 1)
    rows = [matrix[SUB * i : SUB * (i + 1), :] for i in range(count)]

    def place(panel, k):
        parts = [panel]
        if k > 0:
            parts = [jnp.zeros((SUB * k, order), F32)] + parts
        if k < count - 1:
            parts = parts + [jnp.zeros((SUB * (count - 1 - k), order), F32)]
        return jnp.concatenate(parts, axis=0)

    block = [across(rows[0], j) for j in range(SUB)]
    beside = [across(rows[1], a) for a in range(SUB)]
    ahead = [across(rows[1], SUB + j) for j in range(SUB)]
    spread_of = {i: [across(rows[i], a) for a in range(SUB)] for i in range(2, 1 + NEAR)}
    for k in range(count):
        base = SUB * k
        inverse = sweep_columns(block, row_at)
        inside = (lane_at >= base) & (lane_at < base + SUB)
        unit = jnp.where(lane_at - base == row_at, 1.0, 0.0)
        pivot_row = jnp.where(inside, unit, rows[k])
        scaled = tree_sum(inverse[b] * down(pivot_row, b) for b in range(SUB))
        if k < count - 1:
            weights = [
                tree_sum(down(inverse[b], a) * beside[b] for b in range(SUB)) for a in range(SUB)
            ]
            block = [
                ahead[j] - tree_sum(beside[a] * down(weights[a], j) for a in range(SUB))
                for j in range(SUB)
            ]
        spread = [down(scaled, a) for a in range(SUB)]
        near = list(range(k + 1, min(count, k + 1 + NEAR)))
        spread_of[k + 1] = beside
        for i in reversed(near):
            rows[i] = jnp.where(inside, 0.0, rows[i]) - tree_sum(
                spread_of[i][a] * spread[a] for a in range(SUB)
            )
        far = [i for i in range(count) if i != k and i not in near]
        left_high, left_mid = split_pair(jnp.concatenate([rows[i] for i in far], axis=0))
        scaled_high = scaled.astype(BF16).astype(F32)
        right_high = place(scaled_high, k).astype(BF16)
        right_mid = place(scaled - scaled_high, k).astype(BF16)
        update = single(
            jnp.concatenate((left_high, left_mid), axis=1),
            jnp.concatenate((right_high, right_high), axis=0),
        ) + single(left_high, right_mid)
        for place_at, i in enumerate(far):
            rows[i] = (
                jnp.where(inside, 0.0, rows[i]) - update[SUB * place_at : SUB * (place_at + 1)]
            )
        rows[k] = scaled
        if k < count - 2:
            after = base + SUB
            beside = [across(rows[k + 2], after + a) for a in range(SUB)]
            ahead = [across(rows[k + 2], after + SUB + j) for j in range(SUB)]
            spread_of = {
                i: [across(rows[i], after + a) for a in range(SUB)]
                for i in range(k + 3, min(count, k + 2 + NEAR))
            }
    return jnp.concatenate(rows, axis=0)


def add_eye(system):
    row_at = lax.broadcasted_iota(jnp.int32, system.shape, 0)
    lane_at = lax.broadcasted_iota(jnp.int32, system.shape, 1)
    return system + jnp.where(row_at == lane_at, 1.0, 0.0)


def capacitance_solve(grams, terms, factor, flipped, rank):
    wide = jnp.concatenate(
        [
            times_factor(gram, factor[side * rank : (side + 1) * rank])
            for side, gram in enumerate(grams)
        ],
        axis=0,
    )
    system = add_eye(factor_times(flipped, wide))
    rights = times_factor(terms, factor)
    corner = system[:rank, rank:]
    inverse = inverse_spd(system[:rank, :rank])
    head = matmul(inverse, corner)
    rest = system[rank:, rank:] - matmul(system[rank:, :rank], head)
    first = rights[:, :rank]
    second = rights[:, rank:] - matmul(first, head)
    lead = matmul(first, inverse)
    low = matmul(second, inverse_spd(rest))
    high = lead - matmul(low, head, NT)
    return times_factor(jnp.concatenate((high, low), axis=1), flipped)


def local_kernel(
    rhs_hbm, leaf_hbm, one_hbm, two_hbm, solved_ref, keep_ref, give_ref,
    rhs_ref, leaf_ref, bases_ref, sems,
):
    rank = one_hbm.shape[1]
    rows = leaf_hbm.shape[0]
    chunk = 2 * rank
    copies = [
        pltpu.make_async_copy(two_hbm, bases_ref.at[:, :rank], sems.at[0]),
        pltpu.make_async_copy(one_hbm, bases_ref.at[:, rank:], sems.at[1]),
        pltpu.make_async_copy(rhs_hbm, rhs_ref, sems.at[2]),
    ] + [
        pltpu.make_async_copy(leaf_hbm.at[at : at + chunk], leaf_ref.at[at : at + chunk], sem)
        for at, sem in ((c * chunk, sems.at[3 + c]) for c in range(rows // chunk))
    ]
    for copy in copies:
        copy.start()
    for copy in copies[:3]:
        copy.wait()
    bases = bases_ref[...]
    left = split_pair(jnp.concatenate((bases.T, rhs_ref[...]), axis=0))
    bases = split_pair(bases)
    solved = None
    for c in range(rows // chunk):
        copies[3 + c].wait()
        at = c * chunk
        part = pair_matmul(
            [piece[:, at : at + chunk] for piece in left], split_pair(leaf_ref[at : at + chunk, :])
        )
        solved = part if solved is None else solved + part
    solved_ref[...] = solved
    products = pair_matmul(split_pair(solved), bases)
    g22 = products[:rank, :rank]
    g12 = products[rank : 2 * rank, :rank]
    g11 = products[rank : 2 * rank, rank:]
    terms = products[2 * rank :]
    row_at = lax.broadcasted_iota(jnp.int32, (rank, rank), 0)
    lane_at = lax.broadcasted_iota(jnp.int32, (rank, rank), 1)
    both = jnp.where(row_at >= lane_at, g22, g11)
    diagonal = jnp.sum(jnp.where(row_at == lane_at, g11, 0.0), axis=0, keepdims=True)
    pad = jnp.broadcast_to(diagonal, (SUB, rank))
    low = jnp.concatenate((both, terms[:, :rank], pad), axis=0)
    high = jnp.concatenate((g12, terms[:, rank:], pad), axis=0)
    upper = lax.axis_index("gy") % 2 == 1
    keep_ref[...] = jnp.where(upper, high, low)
    give_ref[...] = jnp.where(upper, low, high)


def factor_kernel(one_ref, two_ref, *out_refs):
    fine = lax.axis_size("gy")
    count = lax.axis_size("gx") * fine
    flat = lax.axis_index("gx") * fine + lax.axis_index("gy")
    for level, ref in ((1, one_ref), (2, two_ref)):
        block = count // 2**level
        chosen = ref[flat // (2 * block)].astype(F32)
        rank = chosen.shape[0] // 2
        swapped = jnp.concatenate((chosen[rank:], chosen[:rank]), axis=0)
        chosen = jnp.where(flat // block % 2 == 1, swapped, chosen)
        out_refs[2 * level - 2][...] = chosen.astype(BF16)
        out_refs[2 * level - 1][...] = chosen.T.astype(BF16)


def second_kernel(mine_ref, other_ref, factor_ref, flipped_ref, out_ref, update_ref):
    rank = factor_ref.shape[0] // 2
    upper = lax.axis_index("gy") % 2 == 1
    row_at = lax.broadcasted_iota(jnp.int32, (rank, rank), 0)
    lane_at = lax.broadcasted_iota(jnp.int32, (rank, rank), 1)
    g22, coupling, start = [], [], []
    for side in range(2):
        mine, other = mine_ref[side], other_ref[side]
        low = jnp.where(upper, other, mine)
        high = jnp.where(upper, mine, other)
        end = low.shape[0] - SUB
        both = low[:rank]
        mirror = both.T
        diagonal = jnp.broadcast_to(low[end : end + 1], (rank, rank))
        g22.append(jnp.where(row_at >= lane_at, both, mirror))
        g11 = jnp.where(row_at < lane_at, both, jnp.where(row_at == lane_at, diagonal, mirror))
        coupling.append(jnp.concatenate((high[:rank], low[rank:end]), axis=0))
        start.append(jnp.concatenate((g11, high[rank:end]), axis=0))
    terms = jnp.concatenate(coupling, axis=1)
    update = capacitance_solve(g22, terms, factor_ref[...], flipped_ref[...], rank)
    update_ref[...] = update[:, :rank]
    out_ref[...] = start[0] + start[1] - matmul(update, terms[:rank], NT)


def first_kernel(
    mine_ref, other_ref, factor_ref, flipped_ref, update_ref, solved_ref, out_ref
):
    rank = factor_ref.shape[0] // 2
    mine, other = mine_ref[...], other_ref[...]
    terms = jnp.concatenate((mine[rank:], other[rank:]), axis=1)
    outer = capacitance_solve(
        (mine[:rank], other[:rank]), terms, factor_ref[...], flipped_ref[...], rank
    )[:, :rank]
    inner = update_ref[rank:, :] - matmul(outer, update_ref[:rank, :])
    out_ref[...] = solved_ref[2 * rank :, :] - pair_matmul(
        split_pair(jnp.concatenate((inner, outer), axis=1)),
        split_pair(solved_ref[: 2 * rank, :]),
    )


def call(kernel, shapes, *args, vmem=VMEM_BYTES, **options):
    return pl.pallas_call(
        kernel,
        out_shape=[jax.ShapeDtypeStruct(shape, dtype) for shape, dtype in shapes],
        compiler_params=pltpu.CompilerParams(vmem_limit_bytes=vmem),
        **options,
    )(*args)


def body(right_side, leaf_inverse, basis_one, basis_two, factor_one, factor_two):
    rank = basis_one.shape[1]
    rows, width = right_side.shape
    fine_bits = lax.axis_size("gy").bit_length() - 1
    total_bits = fine_bits + lax.axis_size("gx").bit_length() - 1
    two_bits, one_bits = total_bits - 2, total_bits - 1
    half = rank + width + SUB
    solved, keep, give = call(
        local_kernel,
        [((2 * rank + width, rows), F32), ((half, rank), F32), ((half, rank), F32)],
        right_side.T,
        leaf_inverse,
        basis_one,
        basis_two,
        vmem=LOCAL_VMEM_BYTES,
        in_specs=[pl.BlockSpec(memory_space=pl.ANY)] * 4,
        scratch_shapes=[
            pltpu.VMEM((width, rows), F32),
            pltpu.VMEM((rows, rows), F32),
            pltpu.VMEM((rows, 2 * rank), F32),
            pltpu.SemaphoreType.DMA((3 + rows // (2 * rank),)),
        ],
    )
    total = keep + partner(give, "gy", 1)
    factor_1, flipped_1, factor_2, flipped_2 = call(
        factor_kernel, [((2 * rank, 2 * rank), BF16)] * 4, factor_one, factor_two
    )
    factors = (factor_1, flipped_1, factor_2, flipped_2)
    for bit in range(1, fine_bits):
        received = partner(total, "gy", 2**bit)
        if bit == 1:
            received, factors = lax.optimization_barrier((received, factors))
        total = total + received
    factor_1, flipped_1, factor_2, flipped_2 = factors
    for bit in range(two_bits - fine_bits):
        total = total + partner(total, "gx", 2**bit)
    sibling = partner(total, "gx", 2 ** (two_bits - fine_bits))
    mine = jnp.stack((total, sibling))
    other = partner(mine, "gy", 1)
    products, update = call(
        second_kernel, [((rank + width, rank), F32)] * 2, mine, other, factor_2, flipped_2
    )
    others = partner(products, "gx", 2 ** (one_bits - fine_bits))
    (result,) = call(
        first_kernel,
        [((width, rows), F32)],
        products,
        others,
        factor_1,
        flipped_1,
        update,
        solved,
    )
    return result.T


def solution(mesh):
    rows = P(("gx", "gy"), None)
    return jax.shard_map(
        body,
        mesh=mesh,
        in_specs=(rows, rows, rows, rows, P(), P()),
        out_specs=rows,
        check_vma=False,
    )
```

```python
import jax
import jax.numpy as jnp
from jax import lax
from jax.experimental import pallas as pl
from jax.experimental.pallas import tpu as pltpu
from jax.sharding import PartitionSpec as P

F32 = jnp.float32
BF16 = jnp.bfloat16
SUB = 8
NEAR = 2
VMEM_BYTES = 32 * 1024 * 1024
LOCAL_VMEM_BYTES = 54988 * 1024

NN = (((1,), (0,)), ((), ()))
NT = (((1,), (1,)), ((), ()))
TN = (((0,), (0,)), ((), ()))


def partner(value, axis, mask):
    pairs = [(source, source ^ mask) for source in range(lax.axis_size(axis))]
    return lax.ppermute(value, axis, pairs)


def single(left, right, dims=NN):
    return lax.dot_general(left, right, dims, preferred_element_type=F32)


def times_factor(value, factor, dims=NN):
    high, low = split_pair(value)
    return single(high, factor, dims) + single(low, factor, dims)


def factor_times(factor, value):
    high, low = split_pair(value)
    return single(factor, high) + single(factor, low)


def split_pair(value):
    high = value.astype(BF16)
    return high, (value - high.astype(F32)).astype(BF16)


def pair_matmul(left, right, dims=NN):
    return single(left[0], right[0], dims) + (
        single(left[0], right[1], dims) + single(left[1], right[0], dims)
    )


def matmul(left, right, dims=NN):
    return pair_matmul(split_pair(left), split_pair(right), dims)


def tree_sum(terms):
    terms = list(terms)
    while len(terms) > 1:
        terms = [
            terms[i] + terms[i + 1] if i + 1 < len(terms) else terms[i]
            for i in range(0, len(terms), 2)
        ]
    return terms[0]


def across(panel, lane):
    return jnp.broadcast_to(panel[:, lane : lane + 1], panel.shape)


def down(panel, row):
    return jnp.broadcast_to(panel[row : row + 1, :], panel.shape)


def sweep_columns(columns, row_at):
    columns = list(columns)
    for t in range(SUB):
        pivot = columns[t]
        scale = 1.0 / down(pivot, t)
        here = row_at == t
        for j in range(SUB):
            if j != t:
                weight = down(columns[j], t) * scale
                columns[j] = jnp.where(here, weight, columns[j] - pivot * weight)
        columns[t] = jnp.where(here, scale, -(pivot * scale))
    return columns


def inverse_spd(matrix):
    order = matrix.shape[0]
    count = order // SUB
    shape = (SUB, order)
    row_at = lax.broadcasted_iota(jnp.int32, shape, 0)
    lane_at = lax.broadcasted_iota(jnp.int32, shape, 1)
    rows = [matrix[SUB * i : SUB * (i + 1), :] for i in range(count)]

    def place(panel, k):
        parts = [panel]
        if k > 0:
            parts = [jnp.zeros((SUB * k, order), F32)] + parts
        if k < count - 1:
            parts = parts + [jnp.zeros((SUB * (count - 1 - k), order), F32)]
        return jnp.concatenate(parts, axis=0)

    block = [across(rows[0], j) for j in range(SUB)]
    beside = [across(rows[1], a) for a in range(SUB)]
    ahead = [across(rows[1], SUB + j) for j in range(SUB)]
    spread_of = {i: [across(rows[i], a) for a in range(SUB)] for i in range(2, 1 + NEAR)}
    for k in range(count):
        base = SUB * k
        inverse = sweep_columns(block, row_at)
        inside = (lane_at >= base) & (lane_at < base + SUB)
        unit = jnp.where(lane_at - base == row_at, 1.0, 0.0)
        pivot_row = jnp.where(inside, unit, rows[k])
        scaled = tree_sum(inverse[b] * down(pivot_row, b) for b in range(SUB))
        if k < count - 1:
            weights = [
                tree_sum(down(inverse[b], a) * beside[b] for b in range(SUB)) for a in range(SUB)
            ]
            block = [
                ahead[j] - tree_sum(beside[a] * down(weights[a], j) for a in range(SUB))
                for j in range(SUB)
            ]
        spread = [down(scaled, a) for a in range(SUB)]
        near = list(range(k + 1, min(count, k + 1 + NEAR)))
        spread_of[k + 1] = beside
        for i in reversed(near):
            rows[i] = jnp.where(inside, 0.0, rows[i]) - tree_sum(
                spread_of[i][a] * spread[a] for a in range(SUB)
            )
        far = [i for i in range(count) if i != k and i not in near]
        left_high, left_mid = split_pair(jnp.concatenate([rows[i] for i in far], axis=0))
        scaled_high = scaled.astype(BF16).astype(F32)
        right_high = place(scaled_high, k).astype(BF16)
        right_mid = place(scaled - scaled_high, k).astype(BF16)
        update = single(
            jnp.concatenate((left_high, left_mid), axis=1),
            jnp.concatenate((right_high, right_high), axis=0),
        ) + single(left_high, right_mid)
        for place_at, i in enumerate(far):
            rows[i] = (
                jnp.where(inside, 0.0, rows[i]) - update[SUB * place_at : SUB * (place_at + 1)]
            )
        rows[k] = scaled
        if k < count - 2:
            after = base + SUB
            beside = [across(rows[k + 2], after + a) for a in range(SUB)]
            ahead = [across(rows[k + 2], after + SUB + j) for j in range(SUB)]
            spread_of = {
                i: [across(rows[i], after + a) for a in range(SUB)]
                for i in range(k + 3, min(count, k + 2 + NEAR))
            }
    return jnp.concatenate(rows, axis=0)


def add_eye(system):
    row_at = lax.broadcasted_iota(jnp.int32, system.shape, 0)
    lane_at = lax.broadcasted_iota(jnp.int32, system.shape, 1)
    return system + jnp.where(row_at == lane_at, 1.0, 0.0)


def eliminate(grams, factor, flipped, rank):
    wide = jnp.concatenate(
        [
            times_factor(gram, factor[side * rank : (side + 1) * rank])
            for side, gram in enumerate(grams)
        ],
        axis=0,
    )
    system = add_eye(factor_times(flipped, wide))
    inverse = inverse_spd(system[:rank, :rank])
    head = matmul(inverse, system[:rank, rank:])
    return inverse, head, system[rank:, rank:] - matmul(system[rank:, :rank], head)


def local_kernel(
    rhs_hbm, leaf_hbm, one_hbm, two_hbm, solved_ref,
    keep_gram_ref, give_gram_ref, keep_ref, give_ref,
    rhs_ref, leaf_ref, bases_ref, sems,
):
    rank = one_hbm.shape[1]
    rows = leaf_hbm.shape[0]
    chunk = 2 * rank
    copies = [
        pltpu.make_async_copy(two_hbm, bases_ref.at[:, :rank], sems.at[0]),
        pltpu.make_async_copy(one_hbm, bases_ref.at[:, rank:], sems.at[1]),
        pltpu.make_async_copy(rhs_hbm, rhs_ref, sems.at[2]),
    ] + [
        pltpu.make_async_copy(leaf_hbm.at[at : at + chunk], leaf_ref.at[at : at + chunk], sem)
        for at, sem in ((c * chunk, sems.at[3 + c]) for c in range(rows // chunk))
    ]
    for copy in copies:
        copy.start()
    for copy in copies[:3]:
        copy.wait()
    bases = bases_ref[...]
    left = split_pair(jnp.concatenate((bases.T, rhs_ref[...]), axis=0))
    bases = split_pair(bases)
    solved = None
    for c in range(rows // chunk):
        copies[3 + c].wait()
        at = c * chunk
        part = pair_matmul(
            [piece[:, at : at + chunk] for piece in left], split_pair(leaf_ref[at : at + chunk, :])
        )
        solved = part if solved is None else solved + part
    solved_ref[...] = solved
    products = pair_matmul(split_pair(solved), bases)
    half = rank // 2
    gram = products[:rank, :rank]
    low = jnp.concatenate((products[rank : 2 * rank, :rank], products[2 * rank :, :rank]), axis=0)
    high = jnp.concatenate((products[rank : 2 * rank, rank:], products[2 * rank :, rank:]), axis=0)
    upper = lax.axis_index("gy") % 2 == 1
    keep_gram_ref[...] = jnp.where(upper, gram[half:], gram[:half])
    give_gram_ref[...] = jnp.where(upper, gram[:half], gram[half:])
    keep_ref[...] = jnp.where(upper, high, low)
    give_ref[...] = jnp.where(upper, low, high)


def factor_kernel(one_ref, two_ref, *out_refs):
    fine = lax.axis_size("gy")
    count = lax.axis_size("gx") * fine
    flat = lax.axis_index("gx") * fine + lax.axis_index("gy")
    for level, ref in ((1, one_ref), (2, two_ref)):
        block = count // 2**level
        chosen = ref[flat // (2 * block)].astype(F32)
        rank = chosen.shape[0] // 2
        swapped = jnp.concatenate((chosen[rank:], chosen[:rank]), axis=0)
        chosen = jnp.where(flat // block % 2 == 1, swapped, chosen)
        out_refs[2 * level - 2][...] = chosen.astype(BF16)
        out_refs[2 * level - 1][...] = chosen.T.astype(BF16)


def in_order(mine, other):
    upper = lax.axis_index("gy") % 2 == 1
    return jnp.where(upper, other, mine), jnp.where(upper, mine, other)


def second_head_kernel(mine_ref, other_ref, factor_ref, flipped_ref, inverse_ref, head_ref, rest_ref):
    rank = factor_ref.shape[0] // 2
    grams = [
        jnp.concatenate(in_order(mine_ref[side], other_ref[side]), axis=0) for side in range(2)
    ]
    inverse_ref[...], head_ref[...], rest_ref[...] = eliminate(
        grams, factor_ref[...], flipped_ref[...], rank
    )


def inverse_kernel(rest_ref, head_ref, flipped_ref, out_ref, back_ref):
    rank = rest_ref.shape[0]
    back_ref[...] = backward(head_ref[...], flipped_ref[...], rank)
    out_ref[...] = inverse_spd(rest_ref[...])


def backward(head, flipped, rank):
    high, low = split_pair(head)
    return flipped[rank:].astype(F32) - (
        single(high, flipped[:rank], TN) + single(low, flipped[:rank], TN)
    )


def second_tail_kernel(
    mine_ref, other_ref, factor_ref, flipped_ref, inverse_ref, head_ref, inverse_rest_ref,
    back_ref, out_ref, update_ref,
):
    rank = factor_ref.shape[0] // 2
    coupling, start = [], []
    for side in range(2):
        low, high = in_order(mine_ref[side], other_ref[side])
        coupling.append(low)
        start.append(high)
    terms = jnp.concatenate(coupling, axis=1)
    rights = times_factor(terms, factor_ref[...])
    first = rights[:, :rank]
    second = rights[:, rank:] - matmul(first, head_ref[...])
    lead = matmul(first, inverse_ref[...])
    low = matmul(second, inverse_rest_ref[...])
    update = times_factor(lead, flipped_ref[:rank, :]) + matmul(low, back_ref[...])
    update_ref[...] = update[:, :rank]
    out_ref[...] = start[0] + start[1] - matmul(update, terms[:rank], NT)


def correct_kernel(update_ref, solved_ref, thin_ref, bases_ref):
    rank = update_ref.shape[1]
    change = matmul(update_ref[...], solved_ref[:rank, :])
    thin_ref[...] = solved_ref[2 * rank :, :] - change[rank:]
    bases_ref[...] = solved_ref[rank : 2 * rank, :] - change[:rank]


def first_kernel(mine_ref, other_ref, factor_ref, flipped_ref, thin_ref, bases_ref, out_ref):
    rank = factor_ref.shape[0] // 2
    mine, other = mine_ref[...], other_ref[...]
    factor, flipped = factor_ref[...], flipped_ref[:, : factor_ref.shape[0] // 2]
    inverse, head, rest = eliminate((mine[:rank], other[:rank]), factor, flipped_ref[...], rank)
    rights = times_factor(jnp.concatenate((mine[rank:], other[rank:]), axis=1), factor)
    first = rights[:, :rank]
    second = rights[:, rank:] - matmul(first, head)
    bases = split_pair(bases_ref[...])
    outer = times_factor(matmul(first, inverse), flipped[:rank])
    start = thin_ref[...] - pair_matmul(split_pair(outer), bases)
    last = split_pair(pair_matmul(split_pair(backward(head, flipped, rank)), bases))
    low = matmul(second, inverse_spd(rest))
    out_ref[...] = start - pair_matmul(split_pair(low), last)


def call(kernel, shapes, *args, vmem=VMEM_BYTES, **options):
    return pl.pallas_call(
        kernel,
        out_shape=[jax.ShapeDtypeStruct(shape, dtype) for shape, dtype in shapes],
        compiler_params=pltpu.CompilerParams(vmem_limit_bytes=vmem),
        **options,
    )(*args)


def body(right_side, leaf_inverse, basis_one, basis_two, factor_one, factor_two):
    rank = basis_one.shape[1]
    rows, width = right_side.shape
    fine_bits = lax.axis_size("gy").bit_length() - 1
    total_bits = fine_bits + lax.axis_size("gx").bit_length() - 1
    two_bits, one_bits = total_bits - 2, total_bits - 1
    half, tall = (rank // 2, rank), (rank + width, rank)
    solved, keep_gram, give_gram, keep, give = call(
        local_kernel,
        [((2 * rank + width, rows), F32)] + [(half, F32)] * 2 + [(tall, F32)] * 2,
        right_side.T,
        leaf_inverse,
        basis_one,
        basis_two,
        vmem=LOCAL_VMEM_BYTES,
        in_specs=[pl.BlockSpec(memory_space=pl.ANY)] * 4,
        scratch_shapes=[
            pltpu.VMEM((width, rows), F32),
            pltpu.VMEM((rows, rows), F32),
            pltpu.VMEM((rows, 2 * rank), F32),
            pltpu.SemaphoreType.DMA((3 + rows // (2 * rank),)),
        ],
    )
    gram = keep_gram + partner(give_gram, "gy", 1)
    total = keep + partner(give, "gy", 1)
    factors = call(
        factor_kernel, [((2 * rank, 2 * rank), BF16)] * 4, factor_one, factor_two
    )
    stages = [("gy", 2**bit) for bit in range(1, fine_bits)] + [
        ("gx", 2**bit) for bit in range(two_bits - fine_bits)
    ]
    sibling_mask = 2 ** (two_bits - fine_bits)
    for index, (axis, mask) in enumerate(stages):
        received = partner(gram, axis, mask)
        if index == 0:
            received, factors = lax.optimization_barrier((received, factors))
        gram = gram + received
        total = total + partner(total, axis, mask)
    factor_1, flipped_1, factor_2, flipped_2 = factors
    gram = jnp.stack((gram, partner(gram, "gx", sibling_mask)))
    other_gram = partner(gram, "gy", 1)
    other_gram, total = lax.optimization_barrier((other_gram, total))
    received = partner(total, "gx", sibling_mask)
    inverse, head, rest = call(
        second_head_kernel, [((rank, rank), F32)] * 3, gram, other_gram, factor_2, flipped_2
    )
    rest, received = lax.optimization_barrier((rest, received))
    total = jnp.stack((total, received))
    other = partner(total, "gy", 1)
    inverse_rest, back = call(
        inverse_kernel, [((rank, rank), F32), ((rank, 2 * rank), F32)], rest, head, flipped_2
    )
    products, update = call(
        second_tail_kernel,
        [(tall, F32)] * 2,
        total,
        other,
        factor_2,
        flipped_2,
        inverse,
        head,
        inverse_rest,
        back,
    )
    others = partner(products, "gx", 2 ** (one_bits - fine_bits))
    thin, bases = call(
        correct_kernel, [((width, rows), F32), ((rank, rows), F32)], update, solved
    )
    others, thin, bases = lax.optimization_barrier((others, thin, bases))
    (result,) = call(
        first_kernel,
        [((width, rows), F32)],
        products,
        others,
        factor_1,
        flipped_1,
        thin,
        bases,
    )
    return result.T


def solution(mesh):
    rows = P(("gx", "gy"), None)
    return jax.shard_map(
        body,
        mesh=mesh,
        in_specs=(rows, rows, rows, rows, P(), P()),
        out_specs=rows,
        check_vma=False,
    )
```

```python
import jax
import jax.numpy as jnp
from jax import lax
from jax.experimental import pallas as pl
from jax.experimental.pallas import tpu as pltpu
from jax.sharding import PartitionSpec as P

F32 = jnp.float32
BF16 = jnp.bfloat16
SUB = 8
NEAR = 2
VMEM_BYTES = 32 * 1024 * 1024
LOCAL_VMEM_BYTES = 54988 * 1024

NN = (((1,), (0,)), ((), ()))
NT = (((1,), (1,)), ((), ()))
TN = (((0,), (0,)), ((), ()))


def partner(value, axis, mask):
    pairs = [(source, source ^ mask) for source in range(lax.axis_size(axis))]
    return lax.ppermute(value, axis, pairs)


def single(left, right, dims=NN):
    return lax.dot_general(left, right, dims, preferred_element_type=F32)


def times_factor(value, factor, dims=NN):
    high, low = split_pair(value)
    return single(high, factor, dims) + single(low, factor, dims)


def factor_times(factor, value):
    high, low = split_pair(value)
    return single(factor, high) + single(factor, low)


def split_pair(value):
    high = value.astype(BF16)
    return high, (value - high.astype(F32)).astype(BF16)


def pair_matmul(left, right, dims=NN):
    return single(left[0], right[0], dims) + (
        single(left[0], right[1], dims) + single(left[1], right[0], dims)
    )


def matmul(left, right, dims=NN):
    return pair_matmul(split_pair(left), split_pair(right), dims)


def tree_sum(terms):
    terms = list(terms)
    while len(terms) > 1:
        terms = [
            terms[i] + terms[i + 1] if i + 1 < len(terms) else terms[i]
            for i in range(0, len(terms), 2)
        ]
    return terms[0]


def across(panel, lane):
    return jnp.broadcast_to(panel[:, lane : lane + 1], panel.shape)


def down(panel, row):
    return jnp.broadcast_to(panel[row : row + 1, :], panel.shape)


def sweep_columns(columns, row_at):
    columns = list(columns)
    for t in range(SUB):
        pivot = columns[t]
        scale = 1.0 / down(pivot, t)
        here = row_at == t
        for j in range(SUB):
            if j != t:
                weight = down(columns[j], t) * scale
                columns[j] = jnp.where(here, weight, columns[j] - pivot * weight)
        columns[t] = jnp.where(here, scale, -(pivot * scale))
    return columns


def factor_spd(matrix):
    order = matrix.shape[0]
    count = order // SUB
    shape = (SUB, order)
    row_at = lax.broadcasted_iota(jnp.int32, shape, 0)
    lane_at = lax.broadcasted_iota(jnp.int32, shape, 1)
    rows = [matrix[SUB * i : SUB * (i + 1), :] for i in range(count)]

    def place(panel, k):
        parts = [panel]
        if k > 0:
            parts = [jnp.zeros((SUB * k, panel.shape[1]), F32)] + parts
        if k < count - 1:
            parts = parts + [jnp.zeros((SUB * (count - 1 - k), panel.shape[1]), F32)]
        return jnp.concatenate(parts, axis=0)

    lower, upper = [], []
    block = [across(rows[0], j) for j in range(SUB)]
    beside = [across(rows[1], a) for a in range(SUB)]
    ahead = [across(rows[1], SUB + j) for j in range(SUB)]
    spread_of = {i: [across(rows[i], a) for a in range(SUB)] for i in range(2, 1 + NEAR)}
    for k in range(count):
        base = SUB * k
        inverse = sweep_columns(block, row_at)
        inside = (lane_at >= base) & (lane_at < base + SUB)
        unit = jnp.where(lane_at - base == row_at, 1.0, 0.0)
        pivot_row = jnp.where(inside, unit, rows[k])
        scaled = tree_sum(inverse[b] * down(pivot_row, b) for b in range(SUB))
        if k < count - 1:
            weights = [
                tree_sum(down(inverse[b], a) * beside[b] for b in range(SUB)) for a in range(SUB)
            ]
            block = [
                ahead[j] - tree_sum(beside[a] * down(weights[a], j) for a in range(SUB))
                for j in range(SUB)
            ]
        spread = [down(scaled, a) for a in range(SUB)]
        near = list(range(k + 1, min(count, k + 1 + NEAR)))
        spread_of[k + 1] = beside
        for i in reversed(near):
            rows[i] = jnp.where(inside, 0.0, rows[i]) - tree_sum(
                spread_of[i][a] * spread[a] for a in range(SUB)
            )
        far = list(range(k + 1 + NEAR, count))
        if far:
            left = jnp.concatenate([rows[i] for i in far], axis=0)
            left_rest = left - left.astype(BF16).astype(F32)
            right = scaled.astype(BF16).astype(F32)
            both = single(left, place(jnp.concatenate((right, scaled - right), axis=1), k))
            update = both[:, :order] + both[:, order:] + single(left_rest, place(right, k))
            for place_at, i in enumerate(far):
                rows[i] = (
                    jnp.where(inside, 0.0, rows[i]) - update[SUB * place_at : SUB * (place_at + 1)]
                )
        done = lane_at < base + SUB
        lower.append(jnp.where(done, pivot_row, 0.0))
        upper.append(jnp.where(done, scaled, 0.0))
        if k < count - 2:
            after = base + SUB
            beside = [across(rows[k + 2], after + a) for a in range(SUB)]
            ahead = [across(rows[k + 2], after + SUB + j) for j in range(SUB)]
            spread_of = {
                i: [across(rows[i], after + a) for a in range(SUB)]
                for i in range(k + 3, min(count, k + 2 + NEAR))
            }
    return jnp.concatenate(lower, axis=0), jnp.concatenate(upper, axis=0)


def add_eye(system):
    row_at = lax.broadcasted_iota(jnp.int32, system.shape, 0)
    lane_at = lax.broadcasted_iota(jnp.int32, system.shape, 1)
    return system + jnp.where(row_at == lane_at, 1.0, 0.0)


def eliminate(grams, factor, flipped, rank):
    wide = jnp.concatenate(
        [
            times_factor(gram, factor[side * rank : (side + 1) * rank])
            for side, gram in enumerate(grams)
        ],
        axis=0,
    )
    system = add_eye(factor_times(flipped, wide))
    lower, scaled = factor_spd(system[:rank, :rank])
    beside = matmul(jnp.concatenate((lower, scaled), axis=0), system[:rank, rank:])
    rest = system[rank:, rank:] - matmul(beside[:rank], beside[rank:], TN)
    return lower, scaled, beside[rank:], rest


def backward(head, flipped, rank):
    high, low = split_pair(head)
    return flipped[rank:].astype(F32) - (
        single(high, flipped[:rank], TN) + single(low, flipped[:rank], TN)
    )


def local_kernel(
    rhs_hbm, leaf_hbm, one_hbm, two_hbm, solved_ref,
    keep_gram_ref, give_gram_ref, keep_ref, give_ref,
    rhs_ref, leaf_ref, bases_ref, sems,
):
    rank = one_hbm.shape[1]
    rows = leaf_hbm.shape[0]
    chunk = 2 * rank
    copies = [
        pltpu.make_async_copy(two_hbm, bases_ref.at[:, :rank], sems.at[0]),
        pltpu.make_async_copy(one_hbm, bases_ref.at[:, rank:], sems.at[1]),
        pltpu.make_async_copy(rhs_hbm, rhs_ref, sems.at[2]),
    ] + [
        pltpu.make_async_copy(leaf_hbm.at[at : at + chunk], leaf_ref.at[at : at + chunk], sem)
        for at, sem in ((c * chunk, sems.at[3 + c]) for c in range(rows // chunk))
    ]
    for copy in copies:
        copy.start()
    for copy in copies[:3]:
        copy.wait()
    bases = bases_ref[...]
    left = split_pair(jnp.concatenate((bases.T, rhs_ref[...]), axis=0))
    bases = split_pair(bases)
    solved = None
    for c in range(rows // chunk):
        copies[3 + c].wait()
        at = c * chunk
        part = pair_matmul(
            [piece[:, at : at + chunk] for piece in left], split_pair(leaf_ref[at : at + chunk, :])
        )
        solved = part if solved is None else solved + part
    solved_ref[...] = solved
    products = pair_matmul(split_pair(solved), bases)
    half = rank // 2
    gram = products[:rank, :rank]
    low = jnp.concatenate((products[rank : 2 * rank, :rank], products[2 * rank :, :rank]), axis=0)
    high = jnp.concatenate((products[rank : 2 * rank, rank:], products[2 * rank :, rank:]), axis=0)
    upper = lax.axis_index("gy") % 2 == 1
    keep_gram_ref[...] = jnp.where(upper, gram[half:], gram[:half])
    give_gram_ref[...] = jnp.where(upper, gram[:half], gram[half:])
    keep_ref[...] = jnp.where(upper, high, low)
    give_ref[...] = jnp.where(upper, low, high)


def factor_kernel(one_ref, two_ref, *out_refs):
    fine = lax.axis_size("gy")
    count = lax.axis_size("gx") * fine
    flat = lax.axis_index("gx") * fine + lax.axis_index("gy")
    for level, ref in ((1, one_ref), (2, two_ref)):
        block = count // 2**level
        chosen = ref[flat // (2 * block)].astype(F32)
        rank = chosen.shape[0] // 2
        swapped = jnp.concatenate((chosen[rank:], chosen[:rank]), axis=0)
        chosen = jnp.where(flat // block % 2 == 1, swapped, chosen)
        out_refs[2 * level - 2][...] = chosen.astype(BF16)
        out_refs[2 * level - 1][...] = chosen.T.astype(BF16)


def in_order(mine, other):
    upper = lax.axis_index("gy") % 2 == 1
    return jnp.where(upper, other, mine), jnp.where(upper, mine, other)


def second_head_kernel(mine_ref, other_ref, factor_ref, flipped_ref, *out_refs):
    rank = factor_ref.shape[0] // 2
    grams = [
        jnp.concatenate(in_order(mine_ref[side], other_ref[side]), axis=0) for side in range(2)
    ]
    parts = eliminate(grams, factor_ref[...], flipped_ref[...], rank)
    for ref, part in zip(out_refs, parts):
        ref[...] = part


def kernel_of_pair(lower_ref, scaled_ref, beside_ref, rest_ref, flipped_ref, out_ref):
    rank = rest_ref.shape[0]
    flipped = flipped_ref[...]
    head = matmul(lower_ref[...], beside_ref[...], TN)
    back = backward(head, flipped, rank)
    ahead = times_factor(jnp.concatenate((lower_ref[...], scaled_ref[...]), axis=0), flipped[:rank])
    base = matmul(ahead[:rank], ahead[rank:], TN)
    last = matmul(jnp.concatenate(factor_spd(rest_ref[...]), axis=0), back)
    out_ref[...] = base + matmul(last[:rank], last[rank:], TN)


def second_tail_kernel(mine_ref, other_ref, pair_ref, out_ref, update_ref):
    rank = pair_ref.shape[0] // 2
    coupling, start = [], []
    for side in range(2):
        low, high = in_order(mine_ref[side], other_ref[side])
        coupling.append(low)
        start.append(high)
    terms = jnp.concatenate(coupling, axis=1)
    update = matmul(terms, pair_ref[...])
    update_ref[...] = update[:, :rank]
    out_ref[...] = start[0] + start[1] - matmul(update, terms[:rank], NT)


def correct_kernel(update_ref, solved_ref, thin_ref, bases_ref):
    rank = update_ref.shape[1]
    change = matmul(update_ref[...], solved_ref[:rank, :])
    thin_ref[...] = solved_ref[2 * rank :, :] - change[rank:]
    bases_ref[...] = solved_ref[rank : 2 * rank, :] - change[:rank]


def first_kernel(mine_ref, other_ref, factor_ref, flipped_ref, thin_ref, bases_ref, out_ref):
    rank = factor_ref.shape[0] // 2
    mine, other = mine_ref[...], other_ref[...]
    factor, flipped = factor_ref[...], flipped_ref[:, : factor_ref.shape[0] // 2]
    lower, scaled, beside, rest = eliminate(
        (mine[:rank], other[:rank]), factor, flipped_ref[...], rank
    )
    head = matmul(lower, beside, TN)
    rights = times_factor(jnp.concatenate((mine[rank:], other[rank:]), axis=1), factor)
    first = rights[:, :rank]
    second = rights[:, rank:] - matmul(first, head)
    bases = split_pair(bases_ref[...])
    outer = times_factor(matmul(matmul(first, lower, NT), scaled), flipped[:rank])
    start = thin_ref[...] - pair_matmul(split_pair(outer), bases)
    last = pair_matmul(split_pair(backward(head, flipped, rank)), bases)
    lower, scaled = factor_spd(rest)
    out_ref[...] = start - matmul(matmul(second, lower, NT), matmul(scaled, last))


def call(kernel, shapes, *args, vmem=VMEM_BYTES, **options):
    return pl.pallas_call(
        kernel,
        out_shape=[jax.ShapeDtypeStruct(shape, dtype) for shape, dtype in shapes],
        compiler_params=pltpu.CompilerParams(vmem_limit_bytes=vmem),
        **options,
    )(*args)


def body(right_side, leaf_inverse, basis_one, basis_two, factor_one, factor_two):
    rank = basis_one.shape[1]
    rows, width = right_side.shape
    fine_bits = lax.axis_size("gy").bit_length() - 1
    total_bits = fine_bits + lax.axis_size("gx").bit_length() - 1
    two_bits, one_bits = total_bits - 2, total_bits - 1
    half, tall = (rank // 2, rank), (rank + width, rank)
    solved, keep_gram, give_gram, keep, give = call(
        local_kernel,
        [((2 * rank + width, rows), F32)] + [(half, F32)] * 2 + [(tall, F32)] * 2,
        right_side.T,
        leaf_inverse,
        basis_one,
        basis_two,
        vmem=LOCAL_VMEM_BYTES,
        in_specs=[pl.BlockSpec(memory_space=pl.ANY)] * 4,
        scratch_shapes=[
            pltpu.VMEM((width, rows), F32),
            pltpu.VMEM((rows, rows), F32),
            pltpu.VMEM((rows, 2 * rank), F32),
            pltpu.SemaphoreType.DMA((3 + rows // (2 * rank),)),
        ],
    )
    gram = keep_gram + partner(give_gram, "gy", 1)
    total = keep + partner(give, "gy", 1)
    factors = call(
        factor_kernel, [((2 * rank, 2 * rank), BF16)] * 4, factor_one, factor_two
    )
    stages = [("gy", 2**bit) for bit in range(1, fine_bits)] + [
        ("gx", 2**bit) for bit in range(two_bits - fine_bits)
    ]
    sibling_mask = 2 ** (two_bits - fine_bits)
    for index, (axis, mask) in enumerate(stages):
        received = partner(gram, axis, mask)
        if index == 0:
            received, factors = lax.optimization_barrier((received, factors))
        gram = gram + received
        total = total + partner(total, axis, mask)
    factor_1, flipped_1, factor_2, flipped_2 = factors
    gram = jnp.stack((gram, partner(gram, "gx", sibling_mask)))
    other_gram = partner(gram, "gy", 1)
    other_gram, total = lax.optimization_barrier((other_gram, total))
    received = partner(total, "gx", sibling_mask)
    lower, scaled, beside, rest = call(
        second_head_kernel, [((rank, rank), F32)] * 4, gram, other_gram, factor_2, flipped_2
    )
    rest, received = lax.optimization_barrier((rest, received))
    total = jnp.stack((total, received))
    other = partner(total, "gy", 1)
    (pair,) = call(
        kernel_of_pair, [((2 * rank, 2 * rank), F32)], lower, scaled, beside, rest, flipped_2
    )
    products, update = call(second_tail_kernel, [(tall, F32)] * 2, total, other, pair)
    others = partner(products, "gx", 2 ** (one_bits - fine_bits))
    thin, bases = call(
        correct_kernel, [((width, rows), F32), ((rank, rows), F32)], update, solved
    )
    others, thin, bases = lax.optimization_barrier((others, thin, bases))
    (result,) = call(
        first_kernel,
        [((width, rows), F32)],
        products,
        others,
        factor_1,
        flipped_1,
        thin,
        bases,
    )
    return result.T


def solution(mesh):
    rows = P(("gx", "gy"), None)
    return jax.shard_map(
        body,
        mesh=mesh,
        in_specs=(rows, rows, rows, rows, P(), P()),
        out_specs=rows,
        check_vma=False,
    )
```

```python
import jax
import jax.numpy as jnp
from jax import lax
from jax.experimental import pallas as pl
from jax.experimental.pallas import tpu as pltpu
from jax.sharding import PartitionSpec as P

F32 = jnp.float32
BF16 = jnp.bfloat16
SUB = 8
NEAR = 2
VMEM_BYTES = 32 * 1024 * 1024
LOCAL_VMEM_BYTES = 54988 * 1024

NN = (((1,), (0,)), ((), ()))
NT = (((1,), (1,)), ((), ()))
TN = (((0,), (0,)), ((), ()))


def partner(value, axis, mask):
    pairs = [(source, source ^ mask) for source in range(lax.axis_size(axis))]
    return lax.ppermute(value, axis, pairs)


def single(left, right, dims=NN):
    return lax.dot_general(left, right, dims, preferred_element_type=F32)


def times_factor(value, factor, dims=NN):
    high, low = split_pair(value)
    return single(high, factor, dims) + single(low, factor, dims)


def factor_times(factor, value):
    high, low = split_pair(value)
    return single(factor, high) + single(factor, low)


def split_pair(value):
    high = value.astype(BF16)
    return high, (value - high.astype(F32)).astype(BF16)


def pair_matmul(left, right, dims=NN):
    return single(left[0], right[0], dims) + (
        single(left[0], right[1], dims) + single(left[1], right[0], dims)
    )


def matmul(left, right, dims=NN):
    return pair_matmul(split_pair(left), split_pair(right), dims)


def tree_sum(terms):
    terms = list(terms)
    while len(terms) > 1:
        terms = [
            terms[i] + terms[i + 1] if i + 1 < len(terms) else terms[i]
            for i in range(0, len(terms), 2)
        ]
    return terms[0]


def across(panel, lane):
    return jnp.broadcast_to(panel[:, lane : lane + 1], panel.shape)


def down(panel, row):
    return jnp.broadcast_to(panel[row : row + 1, :], panel.shape)


def sweep_columns(columns, row_at):
    columns = list(columns)
    for t in range(SUB):
        pivot = columns[t]
        scale = 1.0 / down(pivot, t)
        here = row_at == t
        for j in range(SUB):
            if j != t:
                weight = down(columns[j], t) * scale
                columns[j] = jnp.where(here, weight, columns[j] - pivot * weight)
        columns[t] = jnp.where(here, scale, -(pivot * scale))
    return columns


def factor_spd(matrix):
    order = matrix.shape[0]
    count = order // SUB
    shape = (SUB, order)
    row_at = lax.broadcasted_iota(jnp.int32, shape, 0)
    lane_at = lax.broadcasted_iota(jnp.int32, shape, 1)
    rows = [matrix[SUB * i : SUB * (i + 1), :] for i in range(count)]

    def place(panel, k):
        parts = [panel]
        if k > 0:
            parts = [jnp.zeros((SUB * k, panel.shape[1]), F32)] + parts
        if k < count - 1:
            parts = parts + [jnp.zeros((SUB * (count - 1 - k), panel.shape[1]), F32)]
        return jnp.concatenate(parts, axis=0)

    lower, upper = [], []
    block = [across(rows[0], j) for j in range(SUB)]
    beside = [across(rows[1], a) for a in range(SUB)]
    ahead = [across(rows[1], SUB + j) for j in range(SUB)]
    spread_of = {i: [across(rows[i], a) for a in range(SUB)] for i in range(2, 1 + NEAR)}
    for k in range(count):
        base = SUB * k
        inverse = sweep_columns(block, row_at)
        inside = (lane_at >= base) & (lane_at < base + SUB)
        unit = jnp.where(lane_at - base == row_at, 1.0, 0.0)
        pivot_row = jnp.where(inside, unit, rows[k])
        scaled = tree_sum(inverse[b] * down(pivot_row, b) for b in range(SUB))
        if k < count - 1:
            weights = [
                tree_sum(down(inverse[b], a) * beside[b] for b in range(SUB)) for a in range(SUB)
            ]
            block = [
                ahead[j] - tree_sum(beside[a] * down(weights[a], j) for a in range(SUB))
                for j in range(SUB)
            ]
        spread = [down(scaled, a) for a in range(SUB)]
        near = list(range(k + 1, min(count, k + 1 + NEAR)))
        spread_of[k + 1] = beside
        for i in reversed(near):
            rows[i] = jnp.where(inside, 0.0, rows[i]) - tree_sum(
                spread_of[i][a] * spread[a] for a in range(SUB)
            )
        far = list(range(k + 1 + NEAR, count))
        if far:
            left = jnp.concatenate([rows[i] for i in far], axis=0)
            left_rest = left - left.astype(BF16).astype(F32)
            right = scaled.astype(BF16).astype(F32)
            both = single(left, place(jnp.concatenate((right, scaled - right), axis=1), k))
            update = both[:, :order] + both[:, order:] + single(left_rest, place(right, k))
            for place_at, i in enumerate(far):
                rows[i] = (
                    jnp.where(inside, 0.0, rows[i]) - update[SUB * place_at : SUB * (place_at + 1)]
                )
        done = lane_at < base + SUB
        lower.append(jnp.where(done, pivot_row, 0.0))
        upper.append(jnp.where(done, scaled, 0.0))
        if k < count - 2:
            after = base + SUB
            beside = [across(rows[k + 2], after + a) for a in range(SUB)]
            ahead = [across(rows[k + 2], after + SUB + j) for j in range(SUB)]
            spread_of = {
                i: [across(rows[i], after + a) for a in range(SUB)]
                for i in range(k + 3, min(count, k + 2 + NEAR))
            }
    return jnp.concatenate(lower, axis=0), jnp.concatenate(upper, axis=0)


def add_eye(system):
    row_at = lax.broadcasted_iota(jnp.int32, system.shape, 0)
    lane_at = lax.broadcasted_iota(jnp.int32, system.shape, 1)
    return system + jnp.where(row_at == lane_at, 1.0, 0.0)


def eliminate(grams, factor, flipped, rank):
    wide = jnp.concatenate(
        [
            times_factor(gram, factor[side * rank : (side + 1) * rank])
            for side, gram in enumerate(grams)
        ],
        axis=0,
    )
    system = add_eye(factor_times(flipped, wide))
    lower, scaled = factor_spd(system[:rank, :rank])
    beside = matmul(jnp.concatenate((lower, scaled), axis=0), system[:rank, rank:])
    rest = system[rank:, rank:] - matmul(beside[:rank], beside[rank:], TN)
    return lower, scaled, beside[rank:], rest


def backward(head, flipped, rank):
    high, low = split_pair(head)
    return flipped[rank:].astype(F32) - (
        single(high, flipped[:rank], TN) + single(low, flipped[:rank], TN)
    )


def local_kernel(
    rhs_hbm, leaf_hbm, one_hbm, two_hbm, solved_ref,
    keep_gram_ref, give_gram_ref, keep_ref, give_ref,
    rhs_ref, leaf_ref, bases_ref, sems,
):
    rank = one_hbm.shape[1]
    rows = leaf_hbm.shape[0]
    chunk = 2 * rank
    copies = [
        pltpu.make_async_copy(two_hbm, bases_ref.at[:, :rank], sems.at[0]),
        pltpu.make_async_copy(one_hbm, bases_ref.at[:, rank:], sems.at[1]),
        pltpu.make_async_copy(rhs_hbm, rhs_ref, sems.at[2]),
    ] + [
        pltpu.make_async_copy(leaf_hbm.at[at : at + chunk], leaf_ref.at[at : at + chunk], sem)
        for at, sem in ((c * chunk, sems.at[3 + c]) for c in range(rows // chunk))
    ]
    for copy in copies:
        copy.start()
    for copy in copies[:3]:
        copy.wait()
    bases = bases_ref[...]
    left = split_pair(jnp.concatenate((bases.T, rhs_ref[...]), axis=0))
    bases = split_pair(bases)
    solved = None
    for c in range(rows // chunk):
        copies[3 + c].wait()
        at = c * chunk
        part = pair_matmul(
            [piece[:, at : at + chunk] for piece in left], split_pair(leaf_ref[at : at + chunk, :])
        )
        solved = part if solved is None else solved + part
    solved_ref[...] = solved
    products = pair_matmul(split_pair(solved), bases)
    half = rank // 2
    gram = products[:rank, :rank]
    low = jnp.concatenate((products[rank : 2 * rank, :rank], products[2 * rank :, :rank]), axis=0)
    high = jnp.concatenate((products[rank : 2 * rank, rank:], products[2 * rank :, rank:]), axis=0)
    upper = lax.axis_index("gy") % 2 == 1
    keep_gram_ref[...] = jnp.where(upper, gram[half:], gram[:half])
    give_gram_ref[...] = jnp.where(upper, gram[:half], gram[half:])
    keep_ref[...] = jnp.where(upper, high, low)
    give_ref[...] = jnp.where(upper, low, high)


def factor_kernel(one_ref, two_ref, *out_refs):
    fine = lax.axis_size("gy")
    count = lax.axis_size("gx") * fine
    flat = lax.axis_index("gx") * fine + lax.axis_index("gy")
    for level, ref in ((1, one_ref), (2, two_ref)):
        block = count // 2**level
        chosen = ref[flat // (2 * block)].astype(F32)
        rank = chosen.shape[0] // 2
        swapped = jnp.concatenate((chosen[rank:], chosen[:rank]), axis=0)
        chosen = jnp.where(flat // block % 2 == 1, swapped, chosen)
        out_refs[2 * level - 2][...] = chosen.astype(BF16)
        out_refs[2 * level - 1][...] = chosen.T.astype(BF16)


def in_order(mine, other):
    upper = lax.axis_index("gy") % 2 == 1
    return jnp.where(upper, other, mine), jnp.where(upper, mine, other)


def second_head_kernel(mine_ref, other_ref, factor_ref, flipped_ref, *out_refs):
    rank = factor_ref.shape[0] // 2
    grams = [
        jnp.concatenate(in_order(mine_ref[side], other_ref[side]), axis=0) for side in range(2)
    ]
    parts = eliminate(grams, factor_ref[...], flipped_ref[...], rank)
    for ref, part in zip(out_refs, parts):
        ref[...] = part


def kernel_of_pair(lower_ref, scaled_ref, beside_ref, rest_ref, flipped_ref, out_ref):
    rank = rest_ref.shape[0]
    flipped = flipped_ref[...]
    head = matmul(lower_ref[...], beside_ref[...], TN)
    back = backward(head, flipped, rank)
    ahead = times_factor(jnp.concatenate((lower_ref[...], scaled_ref[...]), axis=0), flipped[:rank])
    base = matmul(ahead[:rank], ahead[rank:], TN)
    last = matmul(jnp.concatenate(factor_spd(rest_ref[...]), axis=0), back)
    out_ref[...] = base + matmul(last[:rank], last[rank:], TN)


def second_tail_kernel(
    mine_ref, other_ref, sibling_ref, sibling_other_ref, pair_ref, out_ref, update_ref
):
    rank = pair_ref.shape[0] // 2
    coupling, start = [], []
    for mine, other in ((mine_ref, other_ref), (sibling_ref, sibling_other_ref)):
        low, high = in_order(mine[...], other[...])
        coupling.append(low)
        start.append(high)
    terms = jnp.concatenate(coupling, axis=1)
    update = matmul(terms, pair_ref[...])
    update_ref[...] = update[:, :rank]
    out_ref[...] = start[0] + start[1] - matmul(update, terms[:rank], NT)


def correct_kernel(update_ref, solved_ref, thin_ref, bases_ref):
    rank = update_ref.shape[1]
    change = matmul(update_ref[...], solved_ref[:rank, :])
    thin_ref[...] = solved_ref[2 * rank :, :] - change[rank:]
    bases_ref[...] = solved_ref[rank : 2 * rank, :] - change[:rank]


def first_kernel(mine_ref, other_ref, factor_ref, flipped_ref, thin_ref, bases_ref, out_ref):
    rank = factor_ref.shape[0] // 2
    mine, other = mine_ref[...], other_ref[...]
    factor, flipped = factor_ref[...], flipped_ref[:, : factor_ref.shape[0] // 2]
    lower, scaled, beside, rest = eliminate(
        (mine[:rank], other[:rank]), factor, flipped_ref[...], rank
    )
    head = matmul(lower, beside, TN)
    rights = times_factor(jnp.concatenate((mine[rank:], other[rank:]), axis=1), factor)
    first = rights[:, :rank]
    second = rights[:, rank:] - matmul(first, head)
    bases = split_pair(bases_ref[...])
    outer = times_factor(matmul(matmul(first, lower, NT), scaled), flipped[:rank])
    start = thin_ref[...] - pair_matmul(split_pair(outer), bases)
    last = pair_matmul(split_pair(backward(head, flipped, rank)), bases)
    lower, scaled = factor_spd(rest)
    out_ref[...] = start - matmul(matmul(second, lower, NT), matmul(scaled, last))


def call(kernel, shapes, *args, vmem=VMEM_BYTES, **options):
    return pl.pallas_call(
        kernel,
        out_shape=[jax.ShapeDtypeStruct(shape, dtype) for shape, dtype in shapes],
        compiler_params=pltpu.CompilerParams(vmem_limit_bytes=vmem),
        **options,
    )(*args)


def body(right_side, leaf_inverse, basis_one, basis_two, factor_one, factor_two):
    rank = basis_one.shape[1]
    rows, width = right_side.shape
    fine_bits = lax.axis_size("gy").bit_length() - 1
    total_bits = fine_bits + lax.axis_size("gx").bit_length() - 1
    two_bits, one_bits = total_bits - 2, total_bits - 1
    half, tall = (rank // 2, rank), (rank + width, rank)
    solved, keep_gram, give_gram, keep, give = call(
        local_kernel,
        [((2 * rank + width, rows), F32)] + [(half, F32)] * 2 + [(tall, F32)] * 2,
        right_side.T,
        leaf_inverse,
        basis_one,
        basis_two,
        vmem=LOCAL_VMEM_BYTES,
        in_specs=[pl.BlockSpec(memory_space=pl.ANY)] * 4,
        scratch_shapes=[
            pltpu.VMEM((width, rows), F32),
            pltpu.VMEM((rows, rows), F32),
            pltpu.VMEM((rows, 2 * rank), F32),
            pltpu.SemaphoreType.DMA((3 + rows // (2 * rank),)),
        ],
    )
    gram = keep_gram + partner(give_gram, "gy", 1)
    total = keep + partner(give, "gy", 1)
    factors = call(
        factor_kernel, [((2 * rank, 2 * rank), BF16)] * 4, factor_one, factor_two
    )
    stages = [("gy", 2**bit) for bit in range(1, fine_bits)] + [
        ("gx", 2**bit) for bit in range(two_bits - fine_bits)
    ]
    sibling_mask = 2 ** (two_bits - fine_bits)
    for index, (axis, mask) in enumerate(stages):
        received = partner(gram, axis, mask)
        if index == 0:
            received, factors = lax.optimization_barrier((received, factors))
        gram = gram + received
        total = total + partner(total, axis, mask)
    factor_1, flipped_1, factor_2, flipped_2 = factors
    gram = jnp.stack((gram, partner(gram, "gx", sibling_mask)))
    other_gram = partner(gram, "gy", 1)
    lower, scaled, beside, rest = call(
        second_head_kernel, [((rank, rank), F32)] * 4, gram, other_gram, factor_2, flipped_2
    )
    rest, total = lax.optimization_barrier((rest, total))
    received = partner(total, "gx", sibling_mask)
    other = partner(total, "gy", 1)
    (pair,) = call(
        kernel_of_pair, [((2 * rank, 2 * rank), F32)], lower, scaled, beside, rest, flipped_2
    )
    received, pair = lax.optimization_barrier((received, pair))
    total = (total, other, received, partner(received, "gy", 1))
    products, update = call(second_tail_kernel, [(tall, F32)] * 2, *total, pair)
    others = partner(products, "gx", 2 ** (one_bits - fine_bits))
    thin, bases = call(
        correct_kernel, [((width, rows), F32), ((rank, rows), F32)], update, solved
    )
    others, thin, bases = lax.optimization_barrier((others, thin, bases))
    (result,) = call(
        first_kernel,
        [((width, rows), F32)],
        products,
        others,
        factor_1,
        flipped_1,
        thin,
        bases,
    )
    return result.T


def solution(mesh):
    rows = P(("gx", "gy"), None)
    return jax.shard_map(
        body,
        mesh=mesh,
        in_specs=(rows, rows, rows, rows, P(), P()),
        out_specs=rows,
        check_vma=False,
    )
```

```python
import jax
import jax.numpy as jnp
from jax import lax
from jax.experimental import pallas as pl
from jax.experimental.pallas import tpu as pltpu
from jax.sharding import PartitionSpec as P

F32 = jnp.float32
BF16 = jnp.bfloat16
SUB = 8
NEAR = 2
VMEM_BYTES = 32 * 1024 * 1024
LOCAL_VMEM_BYTES = 54988 * 1024

NN = (((1,), (0,)), ((), ()))
NT = (((1,), (1,)), ((), ()))
TN = (((0,), (0,)), ((), ()))


def partner(value, axis, mask):
    pairs = [(source, source ^ mask) for source in range(lax.axis_size(axis))]
    return lax.ppermute(value, axis, pairs)


def single(left, right, dims=NN):
    return lax.dot_general(left, right, dims, preferred_element_type=F32)


def times_factor(value, factor, dims=NN):
    high, low = split_pair(value)
    return single(high, factor, dims) + single(low, factor, dims)


def factor_times(factor, value):
    high, low = split_pair(value)
    return single(factor, high) + single(factor, low)


def split_pair(value):
    high = value.astype(BF16)
    return high, (value - high.astype(F32)).astype(BF16)


def pair_matmul(left, right, dims=NN):
    return single(left[0], right[0], dims) + (
        single(left[0], right[1], dims) + single(left[1], right[0], dims)
    )


def matmul(left, right, dims=NN):
    return pair_matmul(split_pair(left), split_pair(right), dims)


def tree_sum(terms):
    terms = list(terms)
    while len(terms) > 1:
        terms = [
            terms[i] + terms[i + 1] if i + 1 < len(terms) else terms[i]
            for i in range(0, len(terms), 2)
        ]
    return terms[0]


def across(panel, lane):
    return jnp.broadcast_to(panel[:, lane : lane + 1], panel.shape)


def down(panel, row):
    return jnp.broadcast_to(panel[row : row + 1, :], panel.shape)


def sweep_columns(columns, row_at):
    columns = list(columns)
    for t in range(SUB):
        pivot = columns[t]
        scale = 1.0 / down(pivot, t)
        here = row_at == t
        for j in range(SUB):
            if j != t:
                weight = down(columns[j], t) * scale
                columns[j] = jnp.where(here, weight, columns[j] - pivot * weight)
        columns[t] = jnp.where(here, scale, -(pivot * scale))
    return columns


def factor_spd(matrix):
    order = matrix.shape[0]
    count = order // SUB
    shape = (SUB, order)
    row_at = lax.broadcasted_iota(jnp.int32, shape, 0)
    lane_at = lax.broadcasted_iota(jnp.int32, shape, 1)
    rows = [matrix[SUB * i : SUB * (i + 1), :] for i in range(count)]

    def place(panel, k):
        parts = [panel]
        if k > 0:
            parts = [jnp.zeros((SUB * k, panel.shape[1]), F32)] + parts
        if k < count - 1:
            parts = parts + [jnp.zeros((SUB * (count - 1 - k), panel.shape[1]), F32)]
        return jnp.concatenate(parts, axis=0)

    lower, upper = [], []
    block = [across(rows[0], j) for j in range(SUB)]
    beside = [across(rows[1], a) for a in range(SUB)]
    ahead = [across(rows[1], SUB + j) for j in range(SUB)]
    spread_of = {i: [across(rows[i], a) for a in range(SUB)] for i in range(2, 1 + NEAR)}
    for k in range(count):
        base = SUB * k
        inverse = sweep_columns(block, row_at)
        inside = (lane_at >= base) & (lane_at < base + SUB)
        unit = jnp.where(lane_at - base == row_at, 1.0, 0.0)
        pivot_row = jnp.where(inside, unit, rows[k])
        scaled = tree_sum(inverse[b] * down(pivot_row, b) for b in range(SUB))
        if k < count - 1:
            weights = [
                tree_sum(down(inverse[b], a) * beside[b] for b in range(SUB)) for a in range(SUB)
            ]
            block = [
                ahead[j] - tree_sum(beside[a] * down(weights[a], j) for a in range(SUB))
                for j in range(SUB)
            ]
        spread = [down(scaled, a) for a in range(SUB)]
        near = list(range(k + 1, min(count, k + 1 + NEAR)))
        spread_of[k + 1] = beside
        for i in reversed(near):
            rows[i] = jnp.where(inside, 0.0, rows[i]) - tree_sum(
                spread_of[i][a] * spread[a] for a in range(SUB)
            )
        far = list(range(k + 1 + NEAR, count))
        if far:
            left = jnp.concatenate([rows[i] for i in far], axis=0)
            left_rest = left - left.astype(BF16).astype(F32)
            right = scaled.astype(BF16).astype(F32)
            both = single(left, place(jnp.concatenate((right, scaled - right), axis=1), k))
            update = both[:, :order] + both[:, order:] + single(left_rest, place(right, k))
            for place_at, i in enumerate(far):
                rows[i] = (
                    jnp.where(inside, 0.0, rows[i]) - update[SUB * place_at : SUB * (place_at + 1)]
                )
        done = lane_at < base + SUB
        lower.append(jnp.where(done, pivot_row, 0.0))
        upper.append(jnp.where(done, scaled, 0.0))
        if k < count - 2:
            after = base + SUB
            beside = [across(rows[k + 2], after + a) for a in range(SUB)]
            ahead = [across(rows[k + 2], after + SUB + j) for j in range(SUB)]
            spread_of = {
                i: [across(rows[i], after + a) for a in range(SUB)]
                for i in range(k + 3, min(count, k + 2 + NEAR))
            }
    return jnp.concatenate(lower, axis=0), jnp.concatenate(upper, axis=0)


def add_eye(system):
    row_at = lax.broadcasted_iota(jnp.int32, system.shape, 0)
    lane_at = lax.broadcasted_iota(jnp.int32, system.shape, 1)
    return system + jnp.where(row_at == lane_at, 1.0, 0.0)


def eliminate(grams, factor, flipped, rank):
    wide = jnp.concatenate(
        [
            times_factor(gram, factor[side * rank : (side + 1) * rank])
            for side, gram in enumerate(grams)
        ],
        axis=0,
    )
    system = add_eye(factor_times(flipped, wide))
    lower, scaled = factor_spd(system[:rank, :rank])
    beside = matmul(jnp.concatenate((lower, scaled), axis=0), system[:rank, rank:])
    rest = system[rank:, rank:] - matmul(beside[:rank], beside[rank:], TN)
    return lower, scaled, beside[rank:], rest


def backward(head, flipped, rank):
    high, low = split_pair(head)
    return flipped[rank:].astype(F32) - (
        single(high, flipped[:rank], TN) + single(low, flipped[:rank], TN)
    )


def local_kernel(
    rhs_hbm, leaf_hbm, one_hbm, two_hbm, solved_ref,
    keep_gram_ref, give_gram_ref, keep_ref, give_ref,
    rhs_ref, leaf_ref, one_ref, two_ref, sems,
):
    rank = one_hbm.shape[1]
    rows = leaf_hbm.shape[0]
    chunk = 2 * rank
    copies = [
        pltpu.make_async_copy(two_hbm, two_ref, sems.at[0]),
        pltpu.make_async_copy(one_hbm, one_ref, sems.at[1]),
        pltpu.make_async_copy(rhs_hbm, rhs_ref, sems.at[2]),
    ] + [
        pltpu.make_async_copy(leaf_hbm.at[at : at + chunk], leaf_ref.at[at : at + chunk], sem)
        for at, sem in ((c * chunk, sems.at[3 + c]) for c in range(rows // chunk))
    ]
    for copy in copies:
        copy.start()
    for copy in copies[:3]:
        copy.wait()
    bases = jnp.concatenate((two_ref[...], one_ref[...]), axis=1)
    left = split_pair(jnp.concatenate((bases.T, rhs_ref[...]), axis=0))
    bases = split_pair(bases)
    solved = None
    for c in range(rows // chunk):
        copies[3 + c].wait()
        at = c * chunk
        part = pair_matmul(
            [piece[:, at : at + chunk] for piece in left], split_pair(leaf_ref[at : at + chunk, :])
        )
        solved = part if solved is None else solved + part
    solved_ref[...] = solved
    products = pair_matmul(split_pair(solved), bases)
    half = rank // 2
    gram = products[:rank, :rank]
    low = jnp.concatenate((products[rank : 2 * rank, :rank], products[2 * rank :, :rank]), axis=0)
    high = jnp.concatenate((products[rank : 2 * rank, rank:], products[2 * rank :, rank:]), axis=0)
    upper = lax.axis_index("gy") % 2 == 1
    keep_gram_ref[...] = jnp.where(upper, gram[half:], gram[:half])
    give_gram_ref[...] = jnp.where(upper, gram[:half], gram[half:])
    keep_ref[...] = jnp.where(upper, high, low)
    give_ref[...] = jnp.where(upper, low, high)


def factor_kernel(one_ref, two_ref, *out_refs):
    fine = lax.axis_size("gy")
    count = lax.axis_size("gx") * fine
    flat = lax.axis_index("gx") * fine + lax.axis_index("gy")
    for level, ref in ((1, one_ref), (2, two_ref)):
        block = count // 2**level
        chosen = ref[flat // (2 * block)].astype(F32)
        rank = chosen.shape[0] // 2
        swapped = jnp.concatenate((chosen[rank:], chosen[:rank]), axis=0)
        chosen = jnp.where(flat // block % 2 == 1, swapped, chosen)
        out_refs[2 * level - 2][...] = chosen.astype(BF16)
        out_refs[2 * level - 1][...] = chosen.T.astype(BF16)


def in_order(mine, other):
    upper = lax.axis_index("gy") % 2 == 1
    return jnp.where(upper, other, mine), jnp.where(upper, mine, other)


def second_head_kernel(mine_ref, other_ref, factor_ref, flipped_ref, *out_refs):
    rank = factor_ref.shape[0] // 2
    grams = [
        jnp.concatenate(in_order(mine_ref[side], other_ref[side]), axis=0) for side in range(2)
    ]
    parts = eliminate(grams, factor_ref[...], flipped_ref[...], rank)
    for ref, part in zip(out_refs, parts):
        ref[...] = part


def kernel_of_pair(lower_ref, scaled_ref, beside_ref, rest_ref, flipped_ref, out_ref):
    rank = rest_ref.shape[0]
    flipped = flipped_ref[...]
    head = matmul(lower_ref[...], beside_ref[...], TN)
    back = backward(head, flipped, rank)
    ahead = times_factor(jnp.concatenate((lower_ref[...], scaled_ref[...]), axis=0), flipped[:rank])
    base = matmul(ahead[:rank], ahead[rank:], TN)
    last = matmul(jnp.concatenate(factor_spd(rest_ref[...]), axis=0), back)
    out_ref[...] = base + matmul(last[:rank], last[rank:], TN)


def second_tail_kernel(
    mine_ref, other_ref, sibling_ref, sibling_other_ref, pair_ref, out_ref, update_ref
):
    rank = pair_ref.shape[0] // 2
    coupling, start = [], []
    for mine, other in ((mine_ref, other_ref), (sibling_ref, sibling_other_ref)):
        low, high = in_order(mine[...], other[...])
        coupling.append(low)
        start.append(high)
    terms = jnp.concatenate(coupling, axis=1)
    update = matmul(terms, pair_ref[...])
    update_ref[...] = update[:, :rank]
    out_ref[...] = start[0] + start[1] - matmul(update, terms[:rank], NT)


def correct_kernel(update_ref, solved_ref, thin_ref, bases_ref):
    rank = update_ref.shape[1]
    change = matmul(update_ref[...], solved_ref[:rank, :])
    thin_ref[...] = solved_ref[2 * rank :, :] - change[rank:]
    bases_ref[...] = solved_ref[rank : 2 * rank, :] - change[:rank]


def first_kernel(mine_ref, other_ref, factor_ref, flipped_ref, thin_ref, bases_ref, out_ref):
    rank = factor_ref.shape[0] // 2
    mine, other = mine_ref[...], other_ref[...]
    factor, flipped = factor_ref[...], flipped_ref[:, : factor_ref.shape[0] // 2]
    lower, scaled, beside, rest = eliminate(
        (mine[:rank], other[:rank]), factor, flipped_ref[...], rank
    )
    head = matmul(lower, beside, TN)
    rights = times_factor(jnp.concatenate((mine[rank:], other[rank:]), axis=1), factor)
    first = rights[:, :rank]
    second = rights[:, rank:] - matmul(first, head)
    bases = split_pair(bases_ref[...])
    outer = times_factor(matmul(matmul(first, lower, NT), scaled), flipped[:rank])
    start = thin_ref[...] - pair_matmul(split_pair(outer), bases)
    last = pair_matmul(split_pair(backward(head, flipped, rank)), bases)
    lower, scaled = factor_spd(rest)
    out_ref[...] = start - matmul(matmul(second, lower, NT), matmul(scaled, last))


def call(kernel, shapes, *args, vmem=VMEM_BYTES, **options):
    return pl.pallas_call(
        kernel,
        out_shape=[jax.ShapeDtypeStruct(shape, dtype) for shape, dtype in shapes],
        compiler_params=pltpu.CompilerParams(vmem_limit_bytes=vmem),
        **options,
    )(*args)


def body(right_side, leaf_inverse, basis_one, basis_two, factor_one, factor_two):
    rank = basis_one.shape[1]
    rows, width = right_side.shape
    fine_bits = lax.axis_size("gy").bit_length() - 1
    total_bits = fine_bits + lax.axis_size("gx").bit_length() - 1
    two_bits, one_bits = total_bits - 2, total_bits - 1
    half, tall = (rank // 2, rank), (rank + width, rank)
    solved, keep_gram, give_gram, keep, give = call(
        local_kernel,
        [((2 * rank + width, rows), F32)] + [(half, F32)] * 2 + [(tall, F32)] * 2,
        right_side.T,
        leaf_inverse,
        basis_one,
        basis_two,
        vmem=LOCAL_VMEM_BYTES,
        in_specs=[pl.BlockSpec(memory_space=pl.ANY)] * 4,
        scratch_shapes=[
            pltpu.VMEM((width, rows), F32),
            pltpu.VMEM((rows, rows), F32),
            pltpu.VMEM((rows, rank), F32),
            pltpu.VMEM((rows, rank), F32),
            pltpu.SemaphoreType.DMA((3 + rows // (2 * rank),)),
        ],
    )
    gram = keep_gram + partner(give_gram, "gy", 1)
    total = keep + partner(give, "gy", 1)
    factors = call(
        factor_kernel, [((2 * rank, 2 * rank), BF16)] * 4, factor_one, factor_two
    )
    stages = [("gy", 2**bit) for bit in range(1, fine_bits)] + [
        ("gx", 2**bit) for bit in range(two_bits - fine_bits)
    ]
    sibling_mask = 2 ** (two_bits - fine_bits)
    for index, (axis, mask) in enumerate(stages):
        received = partner(gram, axis, mask)
        if index == 0:
            received, factors = lax.optimization_barrier((received, factors))
        gram = gram + received
        total = total + partner(total, axis, mask)
    factor_1, flipped_1, factor_2, flipped_2 = factors
    gram = jnp.stack((gram, partner(gram, "gx", sibling_mask)))
    other_gram = partner(gram, "gy", 1)
    lower, scaled, beside, rest = call(
        second_head_kernel, [((rank, rank), F32)] * 4, gram, other_gram, factor_2, flipped_2
    )
    rest, total = lax.optimization_barrier((rest, total))
    received = partner(total, "gx", sibling_mask)
    other = partner(total, "gy", 1)
    (pair,) = call(
        kernel_of_pair, [((2 * rank, 2 * rank), F32)], lower, scaled, beside, rest, flipped_2
    )
    received, pair = lax.optimization_barrier((received, pair))
    total = (total, other, received, partner(received, "gy", 1))
    products, update = call(second_tail_kernel, [(tall, F32)] * 2, *total, pair)
    others = partner(products, "gx", 2 ** (one_bits - fine_bits))
    thin, bases = call(
        correct_kernel, [((width, rows), F32), ((rank, rows), F32)], update, solved
    )
    others, thin, bases = lax.optimization_barrier((others, thin, bases))
    (result,) = call(
        first_kernel,
        [((width, rows), F32)],
        products,
        others,
        factor_1,
        flipped_1,
        thin,
        bases,
    )
    return result.T


def solution(mesh):
    rows = P(("gx", "gy"), None)
    return jax.shard_map(
        body,
        mesh=mesh,
        in_specs=(rows, rows, rows, rows, P(), P()),
        out_specs=rows,
        check_vma=False,
    )
```

```python
import jax
import jax.numpy as jnp
from jax import lax
from jax.experimental import pallas as pl
from jax.experimental.pallas import tpu as pltpu
from jax.sharding import PartitionSpec as P

F32 = jnp.float32
BF16 = jnp.bfloat16
SUB = 8
NEAR = 2
VMEM_BYTES = 32 * 1024 * 1024
LOCAL_VMEM_BYTES = 54988 * 1024

NN = (((1,), (0,)), ((), ()))
NT = (((1,), (1,)), ((), ()))
TN = (((0,), (0,)), ((), ()))


def partner(value, axis, mask):
    pairs = [(source, source ^ mask) for source in range(lax.axis_size(axis))]
    return lax.ppermute(value, axis, pairs)


def single(left, right, dims=NN):
    return lax.dot_general(left, right, dims, preferred_element_type=F32)


def times_factor(value, factor, dims=NN):
    high, low = split_pair(value)
    return single(high, factor, dims) + single(low, factor, dims)


def factor_times(factor, value):
    high, low = split_pair(value)
    return single(factor, high) + single(factor, low)


def split_pair(value):
    high = value.astype(BF16)
    return high, (value - high.astype(F32)).astype(BF16)


def pair_matmul(left, right, dims=NN):
    return single(left[0], right[0], dims) + (
        single(left[0], right[1], dims) + single(left[1], right[0], dims)
    )


def matmul(left, right, dims=NN):
    return pair_matmul(split_pair(left), split_pair(right), dims)


def tree_sum(terms):
    terms = list(terms)
    while len(terms) > 1:
        terms = [
            terms[i] + terms[i + 1] if i + 1 < len(terms) else terms[i]
            for i in range(0, len(terms), 2)
        ]
    return terms[0]


def across(panel, lane):
    return jnp.broadcast_to(panel[:, lane : lane + 1], panel.shape)


def down(panel, row):
    return jnp.broadcast_to(panel[row : row + 1, :], panel.shape)


def sweep_columns(columns, row_at):
    columns = list(columns)
    for t in range(SUB):
        pivot = columns[t]
        scale = 1.0 / down(pivot, t)
        here = row_at == t
        for j in range(SUB):
            if j != t:
                weight = down(columns[j], t) * scale
                columns[j] = jnp.where(here, weight, columns[j] - pivot * weight)
        columns[t] = jnp.where(here, scale, -(pivot * scale))
    return columns


def factor_spd(matrix):
    order = matrix.shape[0]
    count = order // SUB
    shape = (SUB, order)
    row_at = lax.broadcasted_iota(jnp.int32, shape, 0)
    lane_at = lax.broadcasted_iota(jnp.int32, shape, 1)
    rows = [matrix[SUB * i : SUB * (i + 1), :] for i in range(count)]

    def place(panel, k):
        parts = [panel]
        if k > 0:
            parts = [jnp.zeros((SUB * k, panel.shape[1]), F32)] + parts
        if k < count - 1:
            parts = parts + [jnp.zeros((SUB * (count - 1 - k), panel.shape[1]), F32)]
        return jnp.concatenate(parts, axis=0)

    lower, upper = [], []
    block = [across(rows[0], j) for j in range(SUB)]
    beside = [across(rows[1], a) for a in range(SUB)]
    ahead = [across(rows[1], SUB + j) for j in range(SUB)]
    spread_of = {i: [across(rows[i], a) for a in range(SUB)] for i in range(2, 1 + NEAR)}
    for k in range(count):
        base = SUB * k
        inverse = sweep_columns(block, row_at)
        inside = (lane_at >= base) & (lane_at < base + SUB)
        unit = jnp.where(lane_at - base == row_at, 1.0, 0.0)
        pivot_row = jnp.where(inside, unit, rows[k])
        scaled = tree_sum(inverse[b] * down(pivot_row, b) for b in range(SUB))
        if k < count - 1:
            weights = [
                tree_sum(down(inverse[b], a) * beside[b] for b in range(SUB)) for a in range(SUB)
            ]
            block = [
                ahead[j] - tree_sum(beside[a] * down(weights[a], j) for a in range(SUB))
                for j in range(SUB)
            ]
        spread = [down(scaled, a) for a in range(SUB)]
        near = list(range(k + 1, min(count, k + 1 + NEAR)))
        spread_of[k + 1] = beside
        for i in reversed(near):
            rows[i] = jnp.where(inside, 0.0, rows[i]) - tree_sum(
                spread_of[i][a] * spread[a] for a in range(SUB)
            )
        far = list(range(k + 1 + NEAR, count))
        if far:
            left = jnp.concatenate([rows[i] for i in far], axis=0)
            left_rest = left - left.astype(BF16).astype(F32)
            right = scaled.astype(BF16).astype(F32)
            both = single(left, place(jnp.concatenate((right, scaled - right), axis=1), k))
            update = both[:, :order] + both[:, order:] + single(left_rest, place(right, k))
            for place_at, i in enumerate(far):
                rows[i] = (
                    jnp.where(inside, 0.0, rows[i]) - update[SUB * place_at : SUB * (place_at + 1)]
                )
        done = lane_at < base + SUB
        lower.append(jnp.where(done, pivot_row, 0.0))
        upper.append(jnp.where(done, scaled, 0.0))
        if k < count - 2:
            after = base + SUB
            beside = [across(rows[k + 2], after + a) for a in range(SUB)]
            ahead = [across(rows[k + 2], after + SUB + j) for j in range(SUB)]
            spread_of = {
                i: [across(rows[i], after + a) for a in range(SUB)]
                for i in range(k + 3, min(count, k + 2 + NEAR))
            }
    return jnp.concatenate(lower, axis=0), jnp.concatenate(upper, axis=0)


def add_eye(system):
    row_at = lax.broadcasted_iota(jnp.int32, system.shape, 0)
    lane_at = lax.broadcasted_iota(jnp.int32, system.shape, 1)
    return system + jnp.where(row_at == lane_at, 1.0, 0.0)


def eliminate(grams, factor, flipped, rank):
    wide = jnp.concatenate(
        [
            times_factor(gram, factor[side * rank : (side + 1) * rank])
            for side, gram in enumerate(grams)
        ],
        axis=0,
    )
    system = add_eye(factor_times(flipped, wide))
    lower, scaled = factor_spd(system[:rank, :rank])
    beside = matmul(jnp.concatenate((lower, scaled), axis=0), system[:rank, rank:])
    rest = system[rank:, rank:] - matmul(beside[:rank], beside[rank:], TN)
    return lower, scaled, beside[rank:], rest


def backward(head, flipped, rank):
    high, low = split_pair(head)
    return flipped[rank:].astype(F32) - (
        single(high, flipped[:rank], TN) + single(low, flipped[:rank], TN)
    )


def local_kernel(
    rhs_hbm, leaf_hbm, one_hbm, two_hbm, solved_ref,
    keep_gram_ref, give_gram_ref, keep_ref, give_ref,
    rhs_ref, leaf_ref, bases_ref, sems,
):
    rank = one_hbm.shape[1]
    rows = leaf_hbm.shape[0]
    chunk = 2 * rank
    copies = [
        pltpu.make_async_copy(two_hbm, bases_ref.at[:, :rank], sems.at[0]),
        pltpu.make_async_copy(one_hbm, bases_ref.at[:, rank:], sems.at[1]),
        pltpu.make_async_copy(rhs_hbm, rhs_ref, sems.at[2]),
    ] + [
        pltpu.make_async_copy(leaf_hbm.at[at : at + chunk], leaf_ref.at[at : at + chunk], sem)
        for at, sem in ((c * chunk, sems.at[3 + c]) for c in range(rows // chunk))
    ]
    for copy in copies:
        copy.start()
    for copy in copies[:3]:
        copy.wait()
    bases = bases_ref[...]
    left = split_pair(jnp.concatenate((bases.T, rhs_ref[...]), axis=0))
    bases = split_pair(bases)
    solved = None
    for c in range(rows // chunk):
        copies[3 + c].wait()
        at = c * chunk
        part = pair_matmul(
            [piece[:, at : at + chunk] for piece in left], split_pair(leaf_ref[at : at + chunk, :])
        )
        solved = part if solved is None else solved + part
    solved_ref[...] = solved
    products = pair_matmul(split_pair(solved), bases)
    half = rank // 2
    gram = products[:rank, :rank]
    low = jnp.concatenate((products[rank : 2 * rank, :rank], products[2 * rank :, :rank]), axis=0)
    high = jnp.concatenate((products[rank : 2 * rank, rank:], products[2 * rank :, rank:]), axis=0)
    upper = lax.axis_index("gy") % 2 == 1
    keep_gram_ref[...] = jnp.where(upper, gram[half:], gram[:half])
    give_gram_ref[...] = jnp.where(upper, gram[:half], gram[half:])
    keep_ref[...] = jnp.where(upper, high, low)
    give_ref[...] = jnp.where(upper, low, high)


def factor_kernel(one_ref, two_ref, *out_refs):
    fine = lax.axis_size("gy")
    count = lax.axis_size("gx") * fine
    flat = lax.axis_index("gx") * fine + lax.axis_index("gy")
    for level, ref in ((1, one_ref), (2, two_ref)):
        block = count // 2**level
        chosen = ref[flat // (2 * block)].astype(F32)
        rank = chosen.shape[0] // 2
        swapped = jnp.concatenate((chosen[rank:], chosen[:rank]), axis=0)
        chosen = jnp.where(flat // block % 2 == 1, swapped, chosen)
        out_refs[2 * level - 2][...] = chosen.astype(BF16)
        out_refs[2 * level - 1][...] = chosen.T.astype(BF16)


def in_order(mine, other):
    upper = lax.axis_index("gy") % 2 == 1
    return jnp.where(upper, other, mine), jnp.where(upper, mine, other)


def second_head_kernel(mine_ref, other_ref, factor_ref, flipped_ref, *out_refs):
    rank = factor_ref.shape[0] // 2
    grams = [
        jnp.concatenate(in_order(mine_ref[side], other_ref[side]), axis=0) for side in range(2)
    ]
    parts = eliminate(grams, factor_ref[...], flipped_ref[...], rank)
    for ref, part in zip(out_refs, parts):
        ref[...] = part


def kernel_of_pair(lower_ref, scaled_ref, beside_ref, rest_ref, flipped_ref, out_ref):
    rank = rest_ref.shape[0]
    flipped = flipped_ref[...]
    head = matmul(lower_ref[...], beside_ref[...], TN)
    back = backward(head, flipped, rank)
    ahead = times_factor(jnp.concatenate((lower_ref[...], scaled_ref[...]), axis=0), flipped[:rank])
    base = matmul(ahead[:rank], ahead[rank:], TN)
    last = matmul(jnp.concatenate(factor_spd(rest_ref[...]), axis=0), back)
    out_ref[...] = base + matmul(last[:rank], last[rank:], TN)


def second_tail_kernel(
    mine_ref, other_ref, sibling_ref, sibling_other_ref, pair_ref, out_ref, update_ref
):
    rank = pair_ref.shape[0] // 2
    coupling, start = [], []
    for mine, other in ((mine_ref, other_ref), (sibling_ref, sibling_other_ref)):
        low, high = in_order(mine[...], other[...])
        coupling.append(low)
        start.append(high)
    terms = jnp.concatenate(coupling, axis=1)
    update = matmul(terms, pair_ref[...])
    update_ref[...] = update[:, :rank]
    out_ref[...] = start[0] + start[1] - matmul(update, terms[:rank], NT)


def correct_kernel(update_ref, solved_ref, thin_ref, bases_ref):
    rank = update_ref.shape[1]
    change = matmul(update_ref[...], solved_ref[:rank, :])
    thin_ref[...] = solved_ref[2 * rank :, :] - change[rank:]
    bases_ref[...] = solved_ref[rank : 2 * rank, :] - change[:rank]


def first_kernel(mine_ref, other_ref, factor_ref, flipped_ref, thin_ref, bases_ref, out_ref):
    rank = factor_ref.shape[0] // 2
    mine, other = mine_ref[...], other_ref[...]
    factor, flipped = factor_ref[...], flipped_ref[:, : factor_ref.shape[0] // 2]
    lower, scaled, beside, rest = eliminate(
        (mine[:rank], other[:rank]), factor, flipped_ref[...], rank
    )
    head = matmul(lower, beside, TN)
    rights = times_factor(jnp.concatenate((mine[rank:], other[rank:]), axis=1), factor)
    first = rights[:, :rank]
    second = rights[:, rank:] - matmul(first, head)
    bases = split_pair(bases_ref[...])
    outer = times_factor(matmul(matmul(first, lower, NT), scaled), flipped[:rank])
    start = thin_ref[...] - pair_matmul(split_pair(outer), bases)
    last = pair_matmul(split_pair(backward(head, flipped, rank)), bases)
    lower, scaled = factor_spd(rest)
    out_ref[...] = start - matmul(matmul(second, lower, NT), matmul(scaled, last))


def call(kernel, shapes, *args, vmem=VMEM_BYTES, **options):
    return pl.pallas_call(
        kernel,
        out_shape=[jax.ShapeDtypeStruct(shape, dtype) for shape, dtype in shapes],
        compiler_params=pltpu.CompilerParams(vmem_limit_bytes=vmem),
        **options,
    )(*args)


def body(right_side, leaf_inverse, basis_one, basis_two, factor_one, factor_two):
    rank = basis_one.shape[1]
    rows, width = right_side.shape
    fine_bits = lax.axis_size("gy").bit_length() - 1
    total_bits = fine_bits + lax.axis_size("gx").bit_length() - 1
    two_bits, one_bits = total_bits - 2, total_bits - 1
    half, tall = (rank // 2, rank), (rank + width, rank)
    solved, keep_gram, give_gram, keep, give = call(
        local_kernel,
        [((2 * rank + width, rows), F32)] + [(half, F32)] * 2 + [(tall, F32)] * 2,
        right_side.T,
        leaf_inverse,
        basis_one,
        basis_two,
        vmem=LOCAL_VMEM_BYTES,
        in_specs=[pl.BlockSpec(memory_space=pl.ANY)] * 4,
        scratch_shapes=[
            pltpu.VMEM((width, rows), F32),
            pltpu.VMEM((rows, rows), F32),
            pltpu.VMEM((rows, 2 * rank), F32),
            pltpu.SemaphoreType.DMA((3 + rows // (2 * rank),)),
        ],
    )
    gram = keep_gram + partner(give_gram, "gy", 1)
    total = keep + partner(give, "gy", 1)
    factors = call(
        factor_kernel, [((2 * rank, 2 * rank), BF16)] * 4, factor_one, factor_two
    )
    stages = [("gy", 2**bit) for bit in range(1, fine_bits)] + [
        ("gx", 2**bit) for bit in range(two_bits - fine_bits)
    ]
    sibling_mask = 2 ** (two_bits - fine_bits)
    for index, (axis, mask) in enumerate(stages):
        received = partner(gram, *stages[-1 - index])
        if index == 0:
            received, factors = lax.optimization_barrier((received, factors))
        gram = gram + received
        total = total + partner(total, axis, mask)
    factor_1, flipped_1, factor_2, flipped_2 = factors
    gram = jnp.stack((gram, partner(gram, "gx", sibling_mask)))
    other_gram = partner(gram, "gy", 1)
    lower, scaled, beside, rest = call(
        second_head_kernel, [((rank, rank), F32)] * 4, gram, other_gram, factor_2, flipped_2
    )
    rest, total = lax.optimization_barrier((rest, total))
    received = partner(total, "gx", sibling_mask)
    other = partner(total, "gy", 1)
    (pair,) = call(
        kernel_of_pair, [((2 * rank, 2 * rank), F32)], lower, scaled, beside, rest, flipped_2
    )
    received, pair = lax.optimization_barrier((received, pair))
    total = (total, other, received, partner(received, "gy", 1))
    products, update = call(second_tail_kernel, [(tall, F32)] * 2, *total, pair)
    others = partner(products, "gx", 2 ** (one_bits - fine_bits))
    thin, bases = call(
        correct_kernel, [((width, rows), F32), ((rank, rows), F32)], update, solved
    )
    others, thin, bases = lax.optimization_barrier((others, thin, bases))
    (result,) = call(
        first_kernel,
        [((width, rows), F32)],
        products,
        others,
        factor_1,
        flipped_1,
        thin,
        bases,
    )
    return result.T


def solution(mesh):
    rows = P(("gx", "gy"), None)
    return jax.shard_map(
        body,
        mesh=mesh,
        in_specs=(rows, rows, rows, rows, P(), P()),
        out_specs=rows,
        check_vma=False,
    )
```
